32 devices in a mesh: dp: 8 (over z, x), blk: 4 (over y, core).
Axes of the slice: x: 2, y: 2, z: 4, core: 2. Of those that a mesh axis runs over, the one named last changes fastest.
Arguments:
- layer_input: bfloat16 [16, 1024, 768], P('dp', 'blk'), may hold values from -6 to 6
- doc_lengths: int32 [16, 8], P('dp'), may hold values from 0 to 1024, as said below
- w_qkv: bfloat16 [768, 2304], replicated, may hold values from -0.21875 to 0.21875
- b_query: float32 [768], replicated, may hold values from -3 to 3
- b_value: float32 [768], replicated, may hold values from -0.3 to 0.3
- w_out: bfloat16 [768, 768], replicated, may hold values from -0.875 to 0.875
- b_out: float32 [768], replicated, may hold values from -3 to 3
- w_fc: bfloat16 [768, 3072], replicated, may hold values from -0.21875 to 0.21875
- b_fc: float32 [3072], replicated, may hold values from -3 to 3
- w_proj: bfloat16 [3072, 768], replicated, may hold values from -0.109375 to 0.109375
- b_proj: float32 [768], replicated, may hold values from -3 to 3
- gain_one: float32 [768], replicated, may hold values from 0.1 to 1.9
- shift_one: float32 [768], replicated, may hold values from -3 to 3
- gain_two: float32 [768], replicated, may hold values from 0.1 to 1.9
- shift_two: float32 [768], replicated, may hold values from -3 to 3
- d_out: bfloat16 [16, 1024, 768], P('dp', 'blk'), may hold values from -6 to 6
Outputs:
- layer_output: bfloat16 [16, 1024, 768], P('dp', 'blk')
- grad_input: float32 [16, 1024, 768], P('dp', 'blk')
- grad_w_qkv: float32 [768, 2304], P('dp', 'blk')
- grad_b_query: float32 [768], P('dp')
- grad_b_value: float32 [768], P('dp')
- grad_w_out: float32 [768, 768], P('dp', 'blk')
- grad_b_out: float32 [768], P('dp')
- grad_w_fc: float32 [768, 3072], P('dp', 'blk')
- grad_b_fc: float32 [3072], P('dp')
- grad_w_proj: float32 [3072, 768], P('dp', 'blk')
- grad_b_proj: float32 [768], P('dp')
- grad_gain_one: float32 [768], P('dp')
- grad_shift_one: float32 [768], P('dp')
- grad_gain_two: float32 [768], P('dp')
- grad_shift_two: float32 [768], P('dp')
The draws below stay inside these ranges and needn't reach their ends.
Inputs may be any that keep to these rules, and one draw needn't show every extreme that they name: `doc_lengths`: entry j of a row is the length of document j of that row (0 allowed); the entries of a row sum to 1024. Among the 2 rows of each index of dp, one row holds a single document of 1024 positions.
All inputs are finite; a program needn't handle non-finite values.
Results may differ from the reference program's by a relative error of at most 0.014.
Values may be sent and summed in bfloat16 or wider, within the bound.
A program may use at most 128 MiB of HBM per device.

```python
import jax
import jax.numpy as jnp
from jax import lax

D = 768
HEADS = 12
HEAD = 64
FF = 3072
ROWS_DEV = 2
DOCS = 8
SEQ = 1024
ROWS = 16


def draw_doc_lengths(key, part):
    key = jax.random.fold_in(key, 11)
    cut_key, row_key, column_key = jax.random.split(key, 3)
    cut_points = jnp.sort(jax.random.randint(cut_key, (ROWS, DOCS - 1), 0, SEQ + 1), axis=1).astype(jnp.int32)
    edges = jnp.concatenate([jnp.zeros((ROWS, 1), jnp.int32), cut_points, jnp.full((ROWS, 1), SEQ, jnp.int32)], axis=1)
    pieces = edges[:, 1:] - edges[:, :-1]
    chosen = jax.random.randint(row_key, (ROWS // ROWS_DEV,), 0, ROWS_DEV)
    single = jnp.arange(ROWS) % ROWS_DEV == jnp.repeat(chosen, ROWS_DEV)
    column = jax.random.randint(column_key, (ROWS,), 0, DOCS)
    whole_row = jnp.where(jnp.arange(DOCS)[None, :] == column[:, None], SEQ, 0).astype(jnp.int32)
    return jnp.where(single[:, None], whole_row, pieces).astype(jnp.int32)


def block_scale(rng, dims, cuts, least, top_value):
    factor_of = 1.0
    for dim, blocks in cuts:
        draws = jax.random.uniform(jax.random.fold_in(jax.random.fold_in(rng, 6), dim), (blocks,), jnp.float32, least / len(cuts), top_value / len(cuts))
        factor_of = factor_of * jnp.repeat(jnp.exp(draws), dims[dim] // blocks).reshape((-1,) + (1,) * (len(dims) - 1 - dim))
    return factor_of


def bell_draw(key, shape, width, bound, cuts=(), dtype=jnp.bfloat16):
    entries = width * jax.random.normal(key, shape, jnp.float32)
    if cuts:
        entries = entries * block_scale(key, shape, cuts, -0.22, 0.18)
    return jnp.clip(entries, -bound, bound).astype(dtype)


def setup_inputs(seed: int = 0) -> dict:
    seeds = jax.random.split(jax.random.key(seed), 17)
    layer_input = bell_draw(seeds[0], (ROWS, SEQ, D), 1.0, 6.0, ((0, 8), (1, 4)))
    doc_lengths = draw_doc_lengths(jax.random.fold_in(seeds[16], 71), 0)
    w_qkv = bell_draw(seeds[2], (D, 3 * D), D ** -0.5, 0.21875)
    b_query = bell_draw(seeds[3], (D,), 0.5, 3.0, (), jnp.float32)
    b_value = bell_draw(seeds[4], (D,), 0.05, 0.3, (), jnp.float32)
    w_out = bell_draw(seeds[5], (D, D), (D // 16) ** -0.5, 0.875)
    b_out = bell_draw(seeds[6], (D,), 0.5, 3.0, (), jnp.float32)
    w_fc = bell_draw(seeds[7], (D, FF), D ** -0.5, 0.21875)
    b_fc = bell_draw(seeds[8], (FF,), 0.5, 3.0, (), jnp.float32)
    w_proj = bell_draw(seeds[9], (FF, D), FF ** -0.5, 0.109375)
    b_proj = bell_draw(seeds[10], (D,), 0.5, 3.0, (), jnp.float32)
    gain_one = jnp.clip(1.0 + 0.18 * jax.random.normal(seeds[11], (D,), jnp.float32), 0.1, 1.9)
    shift_one = bell_draw(seeds[12], (D,), 0.5, 3.0, (), jnp.float32)
    gain_two = jnp.clip(1.0 + 0.18 * jax.random.normal(seeds[13], (D,), jnp.float32), 0.1, 1.9)
    shift_two = bell_draw(seeds[14], (D,), 0.5, 3.0, (), jnp.float32)
    d_out = bell_draw(seeds[15], (ROWS, SEQ, D), 1.0, 6.0, ((0, 8), (1, 4)))
    return {"layer_input": layer_input, "doc_lengths": doc_lengths, "w_qkv": w_qkv, "b_query": b_query, "b_value": b_value, "w_out": w_out, "b_out": b_out, "w_fc": w_fc, "b_fc": b_fc, "w_proj": w_proj, "b_proj": b_proj, "gain_one": gain_one, "shift_one": shift_one, "gain_two": gain_two, "shift_two": shift_two, "d_out": d_out}


@jax.custom_vjp
def low(v):
    return lax.optimization_barrier(v.astype(jnp.bfloat16)).astype(jnp.float32)

@jax.custom_vjp
def low_back(v):
    return v

def low_keep(v):
    return (low(v), None)

def low_pass(kept, grad):
    return (grad,)

def back_keep(v):
    return (v, None)

def back_low(kept, grad):
    return (low(grad),)
low.defvjp(low_keep, low_pass)
low_back.defvjp(back_keep, back_low)
ln_epsilon = 1e-05
gelu_factor = 0.7978845608028654
big_negative = -1e+30

def layer_norm(inputs, gain, shift):
    centre = lax.optimization_barrier(jnp.mean(inputs, axis=-1, keepdims=True))
    centered = inputs - centre
    spread = lax.optimization_barrier(jnp.mean(centered * centered, axis=-1, keepdims=True))
    return centered * lax.rsqrt(spread + ln_epsilon) * gain + shift

def gelu_tanh(inputs):
    return 0.5 * inputs * (1.0 + jnp.tanh(gelu_factor * (inputs + 0.044715 * inputs * inputs * inputs)))

def matmul(left_side, right_side):
    return jnp.dot(left_side, right_side, preferred_element_type=jnp.float32, precision=lax.Precision.HIGHEST)

def layer(inputs, allowed, w_qkv, b_query, b_value, w_out, b_out, w_fc, b_fc, w_proj, b_proj, gain_one, shift_one, gain_two, shift_two):
    seq_length = inputs.shape[0]
    model_width = inputs.shape[1]
    attn_in = low(layer_norm(inputs, gain_one, shift_one))
    projected = matmul(attn_in, w_qkv)
    query = low(low_back(projected[:, :model_width] + b_query)).reshape(seq_length, HEADS, HEAD)
    key_heads = low(low_back(projected[:, model_width:2 * model_width])).reshape(seq_length, HEADS, HEAD)
    value_heads = low(low_back(projected[:, 2 * model_width:] + b_value)).reshape(seq_length, HEADS, HEAD)
    scores = jnp.einsum('qhd,khd->hqk', query, key_heads, precision=lax.Precision.HIGHEST) * HEAD ** (-0.5)
    scores = low_back(scores)
    scores = jnp.where(allowed[None], scores, big_negative)
    attention = jax.nn.softmax(scores, axis=-1)
    mixed_heads = jnp.einsum('hqk,khd->qhd', attention, value_heads, precision=lax.Precision.HIGHEST)
    mixed_heads = low(low_back(mixed_heads.reshape(seq_length, model_width)))
    residual = inputs + low_back(matmul(mixed_heads, w_out) + b_out)
    mlp_in = low(layer_norm(residual, gain_two, shift_two))
    hidden = low_back(matmul(mlp_in, w_fc) + b_fc)
    hidden = low(gelu_tanh(hidden))
    return residual + low_back(matmul(hidden, w_proj) + b_proj)

def reference(layer_input, doc_lengths, w_qkv, b_query, b_value, w_out, b_out, w_fc, b_fc, w_proj, b_proj, gain_one, shift_one, gain_two, shift_two, d_out):
    weights = tuple((member.astype(jnp.float32) for member in (w_qkv, b_query, b_value, w_out, b_out, w_fc, b_fc, w_proj, b_proj, gain_one, shift_one, gain_two, shift_two)))

    def one_row(totals, item):
        row_input, row_lengths, row_grad = item
        doc_ends = jnp.cumsum(row_lengths)
        positions = jnp.arange(SEQ)
        doc_of = lax.optimization_barrier(jnp.sum((doc_ends[None, :] <= positions[:, None]).astype(jnp.int32), axis=-1))
        allowed = (doc_of[:, None] == doc_of[None, :]) & (positions[None, :] <= positions[:, None])

        def forward(inputs, *params):
            return layer(inputs, allowed, *params)
        result, pullback = jax.vjp(forward, row_input.astype(jnp.float32), *weights)
        grads = pullback(row_grad.astype(jnp.float32))
        totals = tuple((total + grad_piece for total, grad_piece in zip(totals, grads[1:])))
        return (totals, (result.astype(jnp.bfloat16), grads[0]))
    start_totals = tuple((jnp.zeros(member.shape, jnp.float32) for member in weights))
    totals, (outputs, input_grads) = lax.scan(one_row, start_totals, (layer_input, doc_lengths, d_out))
    return (outputs, input_grads, totals[0], totals[1], totals[2], totals[3], totals[4], totals[5], totals[6], totals[7], totals[8], totals[9], totals[10], totals[11], totals[12])
```

```python
import functools

import jax
import jax.numpy as jnp
from jax import lax
from jax.experimental import pallas as pl
from jax.experimental.pallas import tpu as pltpu
from jax.sharding import PartitionSpec as P

HEADS = 12
HEAD = 64

ln_epsilon = 1e-05
gelu_factor = 0.7978845608028654
big_negative = -1e30

BF = jnp.bfloat16
F32 = jnp.float32
MESH = pl.DeviceIdType.MESH

SPAN = 256
BLOCKS = 4
SEQ = SPAN * BLOCKS
D = 768
HALF = D // 2
FF = 1536
CHUNK = 512
OWN = 96
EARLY = 56

PA_ORDER = ("x", "zh", "y")
PB_ORDER = ("zh", "y", "x")
FA_ORDER = ("zl", "y", "x", "zh")
FB_ORDER = ("y", "zl", "x", "zh")
WO_ORDER = ("y", "zl", "x")
Q_ORDER = ("x", "zl", "zh")
Q_CHAINS = ((0, 0, 3), (1, 0, 3), (2, 0, 1), (2, 1, 1), (2, 2, 1))


PLACES = (
    [("back", n) for n in range(2)]
    + ["branch"]
    + [("pair", p, i) for p in range(3) for i in (3, 2, 1, 0, -1)]
    + [("input", n) for n in range(2)]
    + ["last"]
)
STEPS = {
    "branch": ["pa", "ve"],
    ("pair", 0, 2): ["ve"],
    ("pair", 1, 2): ["ve"],
    ("pair", 1, 1): ["pb", "fa"],
    ("pair", 1, -1): ["fb", "q0"],
    ("pair", 2, 3): ["ve"],
    ("pair", 2, 2): ["pa", "ve"],
    ("pair", 2, -1): ["wo", "q1", "q0"],
    ("input", 1): ["fb"],
    "last": (
        ["q2a", "q2b", "q2c", "q0", "pa", "pa", "vl", "fb", "wo", "pb", "q1", "fa", "vl", "q0", "q0", "wo"]
        + ["q2a", "q2b", "q2c", "pa", "wo", "q2a", "q2b", "pb", "q2c", "fa", "fb", "q1", "pb", "q1", "pb", "wo"]
        + ["q1", "fa"]
    ),
}


def numbered(extras):
    seen, out = {}, {}
    for place in PLACES:
        names = list(STEPS.get(place, ()))
        if place == "last":
            names += ["ve"] * extras
        out[place] = []
        for name in names:
            out[place].append((name, seen.get(name, 0)))
            seen[name] = seen.get(name, 0) + 1
    return out


def proj_lands(order):
    rows, halves, shapes = D, 2, []
    for axis in order:
        if axis == "zh":
            halves = 1
        else:
            rows //= 2
        shapes.append((halves, rows, HALF))
    return shapes + [(2, OWN, HALF), (OWN, HALF)]


def fc_lands(order):
    rows, cols, shapes = D, D, []
    for axis in order:
        if axis == "y":
            cols //= 2
        else:
            rows //= 2
        shapes.append((rows, cols))
    return shapes


def row_lands(order, cols):
    return [(D >> (n + 1), cols) for n in range(len(order))]


def row_weights(order, last=1):
    return {axis: last << (len(order) - 1 - n) for n, axis in enumerate(order)}


def stats(v):
    centre = jnp.mean(v, axis=-1, keepdims=True)
    centered = v - centre
    inverse = lax.rsqrt(jnp.mean(centered * centered, axis=-1, keepdims=True) + ln_epsilon)
    return centered * inverse, inverse


def norm_back(grad_norm, normed, inverse):
    first = jnp.mean(grad_norm, axis=-1, keepdims=True)
    second = jnp.mean(grad_norm * normed, axis=-1, keepdims=True)
    return inverse * (grad_norm - first - normed * second)


def nn(a, b):
    return jnp.dot(a, b, preferred_element_type=F32)


def nt(a, b):
    return lax.dot_general(a, b, (((1,), (1,)), ((), ())), preferred_element_type=F32)


def mul(i, n):
    return pl.multiple_of(i * n, n)


def loop(n, body):
    def step(i, carry):
        body(i)
        return carry

    lax.fori_loop(0, n, step, 0)


def gelu_both(v):
    square = v * v
    inner = jnp.tanh(v * (gelu_factor + 0.044715 * gelu_factor * square))
    half = 0.5 + 0.5 * inner
    value = v * half
    return value, half + value * ((1.0 - inner) * (gelu_factor + 3.0 * 0.044715 * gelu_factor * square))


def top_of(v):
    while v.shape[0] > 8:
        half = v.shape[0] // 2
        v = jnp.maximum(v[:half], v[half:])
    return v


def base(i):
    return SPAN * (i * (i + 1) // 2)


def scratch(dp):
    extras = max(0, dp.bit_length() - 4)
    vm = pltpu.VMEM
    shapes = dict(
        xrow=vm((BLOCKS, SPAN, D), BF),
        drow=vm((BLOCKS, SPAN, D), BF),
        wqkv=vm((D, 3 * HALF), BF),
        wout=vm((D, D), BF),
        wfc=vm((D, FF), BF),
        wproj=vm((FF, D), BF),
        bfc=vm((1, FF), F32),
        ain_t=vm((D, SEQ), BF),
        qn=vm((SEQ, HALF), BF),
        kn=vm((SEQ, HALF), BF),
        vn=vm((SEQ, HALF), BF),
        k_t=vm((128, SEQ), BF),
        v_t=vm((6, HEAD + 16, SEQ), BF),
        start=vm((BLOCKS, 1, SPAN), jnp.int32),
        probs=vm((6, base(4), SPAN), BF),
        linv=vm((6, 1, SEQ), F32),
        delta=vm((6, 1, SEQ), F32),
        o_t=vm((HALF, SEQ), BF),
        mix=vm((2, SEQ, HALF), BF),
        gpj=vm((D, FF), BF),
        gfb=vm((D, D), BF),
        vectors=vm((1, 8 * D + 2 * FF), F32),
        dout_t=vm((D, SEQ), BF),
        hid=vm((SEQ, FF), BF),
        gpre=vm((SEQ, FF), BF),
        obuf=vm((2, SPAN, D), BF),
        oin=vm((2, SPAN, D), BF),
        gbuf=vm((2, SPAN, D), BF),
        gin=vm((2, SPAN, D), BF),
        gres=vm((2, SPAN, D), F32),
        gbr=vm((BLOCKS, SPAN, D), BF),
        dq_t=vm((128, SPAN), F32),
        dk=vm((SEQ, 128), F32),
        dv=vm((SEQ, 128), F32),
        acc_bfc=vm((1, FF), F32),
        acc_qv=vm((2, 1, HALF), F32),
        acc=vm((6, 1, D), F32),
        early=vm((6 + extras, EARLY, 128), F32),
        early_r=vm((5 + extras, EARLY, 128), F32),
        late=vm((dp, 8, 128), F32),
        late_r=vm((dp, 8, 128), F32),
        late_s=vm((8, 128), F32),
        late_q=vm((3, 8, 128), F32),
        late_send=pltpu.SemaphoreType.DMA((dp + 3,)),
        late_recv=pltpu.SemaphoreType.DMA((dp + 3,)),
        local=pltpu.SemaphoreType.DMA((16,)),
        send=pltpu.SemaphoreType.DMA((120,)),
        recv=pltpu.SemaphoreType.DMA((120,)),
    )
    lands = dict(
        pa=proj_lands(PA_ORDER),
        pb=proj_lands(PB_ORDER),
        fa=fc_lands(FA_ORDER),
        fb=fc_lands(FB_ORDER),
        wo=row_lands(WO_ORDER, HALF) + [(2, OWN, HALF), (OWN, HALF)],
    )
    for n, (_, _, units) in enumerate(Q_CHAINS):
        cols = 128 * units
        if n < 2:
            lands[f"q{n}"] = row_lands(Q_ORDER, cols) + [(OWN, cols)] * 3
        else:
            lands[f"q{n}"] = [(4 * OWN, cols), (3, OWN, cols), (3, OWN, cols)]
    for name, sizes in lands.items():
        for n, size in enumerate(sizes):
            shapes[f"{name}_{n}"] = vm(size, BF)
    if extras:
        shapes.update(
            xs_pj=vm((1, HALF // 2, HALF), BF),
            xr_pj=vm((extras, HALF // 2, HALF), BF),
            xs_fc=vm((1, OWN, D), BF),
            xr_fc=vm((extras, OWN, D), BF),
            xs_wo=vm((1, OWN, HALF), BF),
            xr_wo=vm((extras, OWN, HALF), BF),
            xs_q=vm((1, 3, OWN, HALF), BF),
            xr_q=vm((extras, 3, OWN, HALF), BF),
            xc_q=vm((3, OWN, HALF), BF),
            xsend=pltpu.SemaphoreType.DMA((extras, 4)),
            xrecv=pltpu.SemaphoreType.DMA((extras, 4)),
        )
    return shapes


VECTORS = ("b_query", "b_value", "b_out", "b_proj", "gain_one", "shift_one", "gain_two", "shift_two", "b_fc")
INPUTS = ("x_in", "lengths", "w_qkv", "w_out", "w_fc", "w_proj", "d_in") + tuple(n + "_in" for n in VECTORS)
OUTPUTS = ("y_out", "gx_out", "gq_out", "gwo_out", "gfc_out", "gpj_out", "early_out", "late_out")


def kernel(dp, names, *refs):
    r = dict(zip(names, refs))
    a = type("Refs", (), r)
    for n, name in enumerate(VECTORS):
        size = 2 * FF if name == "b_fc" else D
        a.vectors[:, D * n : D * n + size] = r[name + "_in"][...].reshape(1, size)
        setattr(a, name, a.vectors.at[:, D * n : D * n + size])
    d = lax.axis_index("dp")
    b = lax.axis_index("blk")
    y = lax.div(b, 2)
    c = lax.rem(b, 2)
    other = 1 - c

    def bit(weight):
        return lax.rem(lax.div(d, weight), 2)

    def across(weight):
        return (d + weight * (1 - 2 * bit(weight)), b)

    t2, t1, t0 = bit(dp // 2), bit(dp // 4), bit(dp // 8)
    to_core = (d, 2 * y + other)
    to_y = (d, 2 * (1 - y) + c)
    to2, to1, to0 = across(dp // 2), across(dp // 4), across(dp // 8)
    to21 = (to2[0] + to1[0] - d, b)
    to_diagonal = (d, 2 * (1 - y) + other)
    groups = [(lax.rem(d + n, dp), b) for n in range(1, dp)]
    extra = []
    weight = dp // 16
    while weight >= 1:
        extra.append(across(weight))
        weight //= 2

    count = [0]

    def numbers(n):
        count[0] += n
        return count[0] - n

    def remote(src, dst, number, device):
        return pltpu.make_async_remote_copy(
            src_ref=src,
            dst_ref=dst,
            send_sem=a.send.at[number],
            recv_sem=a.recv.at[number],
            device_id=device,
            device_id_type=MESH,
        )

    pending = []

    def post(src, dst, device):
        copy = remote(src, dst, numbers(1), device)
        copy.start()
        pending.append(copy)
        return copy

    barrier = pltpu.get_barrier_semaphore()
    partners = [to_core, to_y, to_diagonal] + groups
    for device in partners:
        pl.semaphore_signal(barrier, inc=1, device_id=device, device_id_type=MESH)
    pl.semaphore_wait(barrier, len(partners))

    far = 2 * (1 - y) + c
    near_p = 2 * y + other
    far_p = 2 * (1 - y) + other
    x_y = post(a.x_in.at[1 - y], a.xrow.at[b], to_y)
    x_c = post(a.x_in.at[y], a.xrow.at[b], to_core)
    x_l = pltpu.make_async_copy(a.x_in.at[y], a.xrow.at[b], a.local.at[0])
    x_l.start()
    half_c = mul(c, HALF)
    loads_qkv = []
    for u in range(3):
        loads_qkv.append(
            pltpu.make_async_copy(
                a.w_qkv.at[:, pl.ds(pl.multiple_of(D * u + c * HALF, 128), HALF)],
                a.wqkv.at[:, pl.ds(HALF * u, HALF)],
                a.local.at[1 + u],
            )
        )
    loads_mlp = [pltpu.make_async_copy(a.w_out, a.wout, a.local.at[4])]
    for h in range(2):
        ff_at = pl.ds(pl.multiple_of(h * FF + c * D, 128), D)
        loads_mlp.append(
            pltpu.make_async_copy(a.w_fc.at[:, ff_at], a.wfc.at[:, pl.ds(h * D, D)], a.local.at[5 + h])
        )
        loads_mlp.append(
            pltpu.make_async_copy(a.w_proj.at[ff_at], a.wproj.at[pl.ds(h * D, D)], a.local.at[7 + h])
        )
        a.bfc[:, h * D : h * D + D] = a.b_fc[:, ff_at]
    d_l = pltpu.make_async_copy(a.d_in.at[y], a.drow.at[b], a.local.at[9])
    for load in loads_qkv + [d_l] + loads_mlp:
        load.start()
    d_y = remote(a.d_in.at[1 - y], a.drow.at[b], numbers(1), to_y)
    pending.append(d_y)
    d_c = post(a.d_in.at[y], a.drow.at[b], to_core)

    position = lax.broadcasted_iota(jnp.int32, (1, SPAN), 1)
    for i in range(BLOCKS):
        begin = jnp.zeros((1, SPAN), jnp.int32)
        total = jnp.int32(0)
        for j in range(8):
            total = total + a.lengths[y, j]
            begin = jnp.where(position + SPAN * i >= total, total, begin)
        a.start[i] = begin
    a.acc[...] = jnp.zeros_like(a.acc)
    a.v_t[:, HEAD:, :] = jnp.ones((6, 16, SEQ), BF)

    for load in loads_qkv:
        load.wait()
    bias_q = a.b_query[:, pl.ds(half_c, HALF)]
    bias_v = a.b_value[:, pl.ds(half_c, HALF)]

    def project(t):
        rows = pl.ds(mul(t, SPAN), SPAN)
        normed, _ = stats(a.xrow[t].astype(F32))
        low = (normed * a.gain_one[...] + a.shift_one[...]).astype(BF)
        out = nn(low, a.wqkv[...])
        a.qn[rows, :] = ((out[:, :HALF] + bias_q).astype(BF).astype(F32) * 0.125).astype(BF)
        values = (out[:, 2 * HALF :] + bias_v).astype(BF)
        turned = values.T
        a.kn[rows, :] = out[:, HALF : 2 * HALF].astype(BF)
        a.vn[rows, :] = values
        for h in range(6):
            a.v_t[h, :HEAD, rows] = turned[HEAD * h : HEAD * h + HEAD]

    def turn(t):
        rows = pl.ds(mul(t, SPAN), SPAN)
        normed, _ = stats(a.xrow[t].astype(F32))
        a.ain_t[:, rows] = (normed * a.gain_one[...] + a.shift_one[...]).astype(BF).T

    def turn_d(t):
        a.dout_t[:, pl.ds(mul(t, SPAN), SPAN)] = a.drow[t].T

    def stack(ref, ts):
        return jnp.concatenate([ref[t] for t in ts], axis=0)

    def stack_rows(ref, spans, cols=slice(None)):
        return jnp.concatenate([ref[rows, cols] for rows in spans], axis=0)

    def spans_of(ts):
        return [pl.ds(mul(t, SPAN), SPAN) for t in ts]

    def grad_hidden(ts, slopes):
        spans = spans_of(ts)
        top = stack(a.drow, ts)
        for f in range(0, FF, CHUNK):
            here = slice(f, f + CHUNK)
            grad = nt(top, a.wproj[here, :])
            if slopes:
                grad = grad * stack_rows(a.gpre, spans, here).astype(F32)
            grad = grad.astype(BF)
            for k, rows in enumerate(spans):
                a.gpre[rows, here] = grad[SPAN * k : SPAN * k + SPAN]

    fwd_x = remote(a.xrow.at[far], a.xrow.at[far], numbers(1), to_core)
    fwd_d = remote(a.drow.at[far], a.drow.at[far], numbers(1), to_core)
    pending += [fwd_x, fwd_d]

    def arrive(s):
        @pl.when(s == 0)
        def _():
            x_l.wait()

        @pl.when(s == 1)
        def _():
            x_c.wait_recv()

        @pl.when(s == 2)
        def _():
            x_y.wait_recv()
            fwd_x.start()
            d_y.start()

        @pl.when(s == 3)
        def _():
            fwd_x.wait_recv()

        far_s = lax.div(s, 2)
        core_s = lax.rem(s, 2)
        t = 2 * (y + far_s * (1 - 2 * y)) + c + core_s * (1 - 2 * c)
        project(t)

        @pl.when(s == 0)
        def _():
            d_l.wait()

        @pl.when(s == 1)
        def _():
            d_c.wait_recv()

            for load in loads_mlp:
                load.wait()

        @pl.when(s < 2)
        def _():
            turn(t)
            turn_d(t)

        @pl.when(s == 1)
        def _():
            grad_hidden((b, near_p), False)

    loop(4, arrive)

    lane = lax.broadcasted_iota(jnp.int32, (1, 128), 1)
    key_index = lax.broadcasted_iota(jnp.int32, (SPAN, SPAN), 0)
    query_index = lax.broadcasted_iota(jnp.int32, (SPAN, SPAN), 1)
    mix_first = numbers(3)

    def mix_copy(p):
        here = a.mix.at[c, :, pl.ds(mul(p, 128), 128)]
        return remote(here, here, mix_first + p, to_core)

    def forward_pair(p):
        cols = pl.ds(mul(p, 128), 128)
        for i in range(BLOCKS):
            rows = slice(SPAN * i, SPAN * i + SPAN)
            keys_n = SPAN * (i + 1)
            pair = a.qn[rows, cols]
            begin = a.start[i]
            for e in range(2):
                head = 2 * p + e
                query = jnp.where(lane // HEAD == e, pair, jnp.zeros_like(pair))
                scores, tops = [], []
                product = nt(a.kn[:keys_n, cols], query)
                for j in range(i + 1):
                    s = product[SPAN * j : SPAN * j + SPAN]
                    ok = key_index + SPAN * j >= begin
                    if j == i:
                        ok = ok & (key_index <= query_index)
                    s = jnp.where(ok, s, big_negative)
                    scores.append(s)
                    tops.append(top_of(s))
                top = tops[0]
                for here in tops[1:]:
                    top = jnp.maximum(top, here)
                top = jnp.max(top, axis=0, keepdims=True)
                for j in range(i + 1):
                    at = base(i) + SPAN * j
                    a.probs[head, at : at + SPAN, :] = jnp.exp(scores[j] - top).astype(BF)

        def mix_head(e):
            head = 2 * p + e
            feats = pl.ds(mul(head, HEAD), HEAD)
            for i in range(BLOCKS):
                rows = slice(SPAN * i, SPAN * i + SPAN)
                keys_n = SPAN * (i + 1)
                out = nn(a.v_t[head, :, :keys_n], a.probs[head, base(i) : base(i) + keys_n, :])
                inverse = 1.0 / out[HEAD : HEAD + 1]
                a.linv[head, :, rows] = inverse
                a.o_t[feats, rows] = (out[:HEAD] * inverse).astype(BF)

        loop(2, mix_head)
        a.mix[c, :, cols] = a.o_t[pl.ds(mul(p, 128), 128), :].T
        mix_copy(p).start()

        @pl.when(p == 2)
        def _():
            d_y.wait_recv()
            fwd_d.start()

    loop(3, forward_pair)
    turn(far)
    turn(far_p)

    for p in range(3):
        mix_copy(p).wait_recv()

    o_first, g_first, b_first = numbers(2), numbers(2), numbers(2)

    def o_copy(s):
        return remote(a.obuf.at[s], a.oin.at[s], o_first + s, to_core)

    def g_copy(s):
        return remote(a.gbuf.at[s], a.gin.at[s], g_first + s, to_core)

    def b_copy(k):
        t = far if k else b
        return remote(a.gbr.at[t], a.gbr.at[t], b_first + k, to_core)

    y_far = remote(a.gbuf.at[1], a.y_out.at[y], numbers(1), to_y)
    y_own = pltpu.make_async_copy(a.gbuf.at[0], a.y_out.at[y], a.local.at[10])

    def blocks_of(g):
        core = other + g * (2 * c - 1)
        return 2 * y + core, 2 * (1 - y) + core

    def layer_pair(g):
        ts = blocks_of(g)
        spans = spans_of(ts)
        mixed = jnp.concatenate([stack_rows(a.mix.at[n], spans) for n in range(2)], axis=1)
        residual = stack(a.xrow, ts).astype(F32) + nn(mixed, a.wout[...]) + a.b_out[...]
        normed, _ = stats(residual)
        low = (normed * a.gain_two[...] + a.shift_two[...]).astype(BF)
        for k, rows in enumerate(spans):
            a.wqkv[:, rows] = low[SPAN * k : SPAN * k + SPAN].T
        for f in range(0, FF, CHUNK):
            here = slice(f, f + CHUNK)
            value, slope = gelu_both(nn(low, a.wfc[:, here]) + a.bfc[:, here])
            value = value.astype(BF)
            a.hid[spans[0], here] = value[:SPAN]
            a.hid[spans[1], here] = value[SPAN:]
            a.gpre[spans[0], here] = (slope[:SPAN] * a.gpre[spans[0], here].astype(F32)).astype(BF)
            a.gpre[spans[1], here] = slope[SPAN:].astype(BF)

        @pl.when(g == 1)
        def _():
            a.gres[0] = residual[:SPAN]
            a.gres[1] = residual[SPAN:]

    loop(2, layer_pair)
    fwd_d.wait_recv()
    turn_d(far)
    turn_d(far_p)

    def part(first, size, n=1):
        return pl.ds(pl.multiple_of(first * size, size), n * size)

    class Chain:
        def __init__(self, stages):
            self.stages = [one_copy(*stage) if len(stage) == 4 else stage for stage in stages]
            self.first = [numbers(len(stage[0])) for stage in self.stages]

        def copies(self, k):
            pieces, _, device = self.stages[k]
            made = [piece() for piece in pieces]
            return [
                remote(piece[0], piece[1], self.first[k] + n, piece[2] if device is None else device)
                for n, piece in enumerate(made)
            ]

        def start(self, k):
            for copy in self.copies(k):
                copy.start()

        def arrive(self, k):
            for copy in self.copies(k):
                copy.wait_recv()

        def step(self, k):
            self.arrive(k)
            keep = self.stages[k][1]
            if keep is not None:
                keep()
            self.start(k + 1)

        def sent(self):
            for k in range(len(self.stages)):
                for copy in self.copies(k):
                    copy.wait_send()

    def plus(keep, came):
        kept, landed = keep(), came()
        kept[...] = kept[...] + landed[...]

    def one_copy(out, land, keep, device):
        landing = land if callable(land) else lambda: land
        return [lambda: (out(), landing())], (lambda: plus(keep, landing)) if keep else None, device

    axes = dict(x=(t0, to0), zl=(t1, to1), zh=(t2, to2), y=(y, to_y))

    def lands_of(name, n):
        return [r[f"{name}_{k}"] for k in range(n)]

    def proj_chain(name, first, order):
        lands = lands_of(name, 5)
        own, last = lands[3], lands[4]

        def at(block, n, h):
            rows = pl.ds(pl.multiple_of(OWN * block, OWN), OWN * n)
            return a.gpj.at[rows, pl.ds(pl.multiple_of(D * h + first, HALF), HALF)]

        stages = []
        start, width, halves = 0, 8, (0, 1)
        for k, axis in enumerate(order):
            mine, device = axes[axis]
            if axis == "zh":
                pairs = [(start, width, 1 - mine, start, mine)]
                halves = (mine,)
            else:
                width //= 2
                gone, kept = start + (1 - mine) * width, start + mine * width
                pairs = [(gone, width, h, kept, h) for h in halves]
                start = kept
            pieces = [
                lambda p=p, k=k, n=n: (at(p[0], p[1], p[2]), lands[k].at[n]) for n, p in enumerate(pairs)
            ]

            def keep(pairs=pairs, k=k, final=k == len(order) - 1, start=start):
                for n, p in enumerate(pairs):
                    plus(lambda: at(p[3], p[1], p[4]), lambda: lands[k].at[n])
                if final:
                    own[c] = at(start + c, 1, t2)[...]

            stages.append((pieces, keep, device))
        stages.append(([lambda: (at(start + other, 1, t2), own.at[c])], None, to_core))
        stages.append(([lambda: (own.at[1 - t1], last)], None, to1))
        return Chain(stages)

    pa = proj_chain("pa", 0, PA_ORDER)
    pb = proj_chain("pb", HALF, PB_ORDER)

    def fc_chain(name, buf, order):
        lands = lands_of(name, 4)

        def at(block, n, w):
            rows = pl.ds(pl.multiple_of(OWN * block, OWN), OWN * n)
            if w is None:
                return buf.at[rows, pl.ds(0, D)]
            return buf.at[rows, part(w, HALF)]

        stages = []
        start, width, side = 0, 8, None
        for k, axis in enumerate(order):
            mine, device = axes[axis]
            if axis == "y":
                gone, kept = (start, width, 1 - y), (start, width, y)
                side = y
            else:
                width //= 2
                gone, kept = (start + (1 - mine) * width, width, side), (start + mine * width, width, side)
                start = kept[0]
            final = k == len(order) - 1
            stages.append(
                (
                    lambda gone=gone: at(*gone),
                    lands[k],
                    None if final else lambda kept=kept: at(*kept),
                    device,
                )
            )
        return Chain(stages), lambda: at(start, 1, y), lands[-1]

    fa, fa_own, fa_last = fc_chain("fa", a.dout_t, FA_ORDER)
    fb, fb_own, fb_last = fc_chain("fb", a.gfb, FB_ORDER)

    def row_stages(at, order, lands):
        stages = []
        start, width = 0, 8
        for k, axis in enumerate(order):
            mine, device = axes[axis]
            width //= 2
            gone, kept = start + (1 - mine) * width, start + mine * width
            stages.append(
                (
                    lambda gone=gone, width=width: at(gone, width),
                    lands[k],
                    lambda kept=kept, width=width: at(kept, width),
                    device,
                )
            )
            start = kept
        return stages, lambda: at(start, 1)

    wo_lands = lands_of("wo", 5)
    wo_stages, wo_own = row_stages(
        lambda block, n: a.wout.at[pl.ds(pl.multiple_of(OWN * block, OWN), OWN * n), pl.ds(0, HALF)],
        WO_ORDER,
        wo_lands,
    )

    def wo_keep():
        kept = wo_own()
        total = (kept[...].astype(F32) + wo_lands[2][...].astype(F32)).astype(BF)
        kept[...] = total
        wo_lands[3][c] = total

    wo = Chain(
        wo_stages[:2]
        + [
            ([lambda: (wo_stages[2][0](), wo_lands[2])], wo_keep, wo_stages[2][3]),
            (wo_own, lambda: wo_lands[3].at[c], None, to_core),
            (lambda: wo_lands[3].at[1 - t2], wo_lands[4], None, to2),
        ]
    )

    def q_chain(n):
        p, first, units = Q_CHAINS[n]
        cols = slice(HALF * p + 128 * first, HALF * p + 128 * (first + units))

        def at(block, n_blocks):
            return a.gpre.at[pl.ds(pl.multiple_of(OWN * block, OWN), OWN * n_blocks), cols]

        def put(core, value):
            a.gq_out[core, p, :, pl.ds(128 * first, 128 * units)] = value

        if n >= 2:
            came_x, came_z, came = lands_of(f"q{n}", 3)
            start = 4 * t0
            own = lambda: at(start + 2 * t1 + t2, 1)
            around = ((2 * (1 - t1) + t2, to1), (2 * t1 + 1 - t2, to2), (2 * (1 - t1) + 1 - t2, to21))

            def keep_z():
                total = own()[...].astype(F32)
                for m in range(3):
                    total = total + came_z[m].astype(F32)
                own()[...] = total.astype(BF)

            def finish():
                chain.arrive(2)
                put(c, own()[...] + came[0])
                put(other, came[1] + came[2])

            chain = Chain(
                [
                    (lambda: at(4 * (1 - t0), 4), came_x, lambda: at(start, 4), to0),
                    (
                        [
                            lambda m=m, block=block, device=device: (at(start + block, 1), came_z.at[m], device)
                            for m, (block, device) in enumerate(around)
                        ],
                        keep_z,
                        None,
                    ),
                    (
                        [
                            lambda m=m, device=device: (own(), came.at[m], device)
                            for m, device in enumerate((to_y, to_core, to_diagonal))
                        ],
                        None,
                        None,
                    ),
                ]
            )
            return chain, finish
        lands = lands_of(f"q{n}", 6)
        stages, own = row_stages(at, Q_ORDER, lands)

        def keep_y():
            lands[5][...] = own()[...] + lands[3][...]

        def finish():
            chain.arrive(4)
            put(c, lands[5][...])
            put(other, lands[4][...])

        chain = Chain(
            stages + [([lambda: (own(), lands[3])], keep_y, to_y), (lambda: lands[5], lands[4], None, to_core)]
        )
        return chain, finish

    def vector_chain(buf, came):
        def stage(n, device):
            def keep():
                buf[n + 1] = buf[n] + came[n]

            return [lambda: (buf.at[n], came.at[n])], keep, device

        return Chain([stage(n, device) for n, device in enumerate([to0, to1, to2, to_y, to_core] + extra)])

    ve = vector_chain(a.early, a.early_r)

    def late_copy(src, dst, number, device):
        return pltpu.make_async_remote_copy(
            src_ref=src,
            dst_ref=dst,
            send_sem=a.late_send.at[number],
            recv_sem=a.late_recv.at[number],
            device_id=device,
            device_id_type=MESH,
        )

    def late_groups():
        return [late_copy(a.late.at[to[0]], a.late_r.at[n + 1], n, to) for n, to in enumerate(groups)]

    def late_row():
        row = (to_core, to_y, to_diagonal)
        return [late_copy(a.late_s, a.late_q.at[n], dp - 1 + n, to) for n, to in enumerate(row)]

    def late_share():
        for copy in late_groups():
            copy.wait_recv()
        total = a.late[d]
        for n in range(1, dp):
            total = total + a.late_r[n]
        a.late_s[...] = total
        for copy in late_row():
            copy.start()

    def late_end():
        for copy in late_row():
            copy.wait_recv()
        a.late_out[...] = a.late_s[...] + a.late_q[0] + a.late_q[1] + a.late_q[2]

    qs = [q_chain(n) for n in range(len(Q_CHAINS))]

    def finish(chain, out, keep, land):
        chain.arrive(len(chain.stages) - 1)
        out[...] = keep[...].astype(F32) + land[...].astype(F32)

    chains = dict(pa=pa, pb=pb, fa=fa, fb=fb, wo=wo, ve=ve)
    last_steps = dict(
        pa=lambda: finish(pa, a.gpj_out.at[pl.ds(0, OWN)], r["pa_3"].at[t1], r["pa_4"]),
        pb=lambda: finish(pb, a.gpj_out.at[pl.ds(OWN, OWN)], r["pb_3"].at[t1], r["pb_4"]),
        fa=lambda: finish(fa, a.gfc_out.at[:, pl.ds(0, HALF)], fa_own(), fa_last),
        fb=lambda: finish(fb, a.gfc_out.at[:, pl.ds(HALF, HALF)], fb_own(), fb_last),
        wo=lambda: finish(wo, a.gwo_out, wo_lands[3].at[t2], wo_lands[4]),
        ve=lambda: (ve.arrive(len(ve.stages) - 1), ve.stages[-1][1]()),
    )
    for n, name in enumerate(("q0", "q1", "q2a", "q2b", "q2c")):
        chains[name], last_steps[name] = qs[n]
    plan = numbered(len(extra))
    assert sum(len(todo) for todo in plan.values()) == 2 + sum(len(chain.stages) for chain in chains.values())

    def steps(place):
        for name, k in plan[place]:
            if name == "vl":
                (late_share, late_end)[k]()
            elif k == len(chains[name].stages) - 1:
                last_steps[name]()
            else:
                chains[name].step(k)

    pa_w, pb_w = (row_weights([x for x in order if x != "zh"], 2) for order in (PA_ORDER, PB_ORDER))
    fa_w, fb_w = (row_weights([x for x in order if x != "y"]) for order in (FA_ORDER, FB_ORDER))
    wo_w, q_w = row_weights(WO_ORDER), row_weights(Q_ORDER)

    for n in range(2):
        h = (1 - t2) if n == 0 else t2
        for w in range(2):
            grad = nn(a.dout_t[HALF * w : HALF * w + HALF, :], a.hid[:, part(h, D)]).astype(BF)
            for i in range(2):
                for e in range(2):
                    piece = grad[2 * OWN * e : 2 * OWN * e + 2 * OWN, HALF * i : HALF * i + HALF]
                    at_a = OWN * (pa_w["x"] * i + pa_w["y"] * w + e)
                    at_b = OWN * (pb_w["x"] * i + pb_w["y"] * w + e)
                    a.gpj[at_a : at_a + OWN, pl.ds(pl.multiple_of(D * h, HALF), HALF)] = piece[:OWN]
                    a.gpj[at_b : at_b + OWN, pl.ds(pl.multiple_of(D * h + HALF, HALF), HALF)] = piece[OWN:]
        if n == 0:
            pb.start(0)
    pa.start(0)

    grad_hidden((far, far_p), True)

    def out_of(g):
        return nn(stack_rows(a.hid, spans_of(blocks_of(g))), a.wproj[...])

    def back_of(g):
        return nt(stack_rows(a.gpre, spans_of(blocks_of(g))), a.wfc[...])

    @pl.when(d >= 0)
    def _():
        out, grad = out_of(0), back_of(0)
        for k in range(2):
            a.obuf[k] = out[SPAN * k : SPAN * k + SPAN].astype(BF)
            o_copy(k).start()
        for k in range(2):
            a.gbuf[k] = grad[SPAN * k : SPAN * k + SPAN].astype(BF)
            g_copy(k).start()

    def weights_fc(n):
        h = lax.rem(n, 2)
        w = lax.div(n, 2)
        ones = jnp.ones((16, SEQ), BF)
        grad = nn(jnp.concatenate([a.wqkv[part(h, HALF), :SEQ], ones], axis=0), a.gpre[:, part(w, D)])
        a.acc_bfc[:, part(w, D)] = grad[HALF : HALF + 1]
        grad = grad.astype(BF)
        for j in range(2):
            for i in range(2):
                piece = grad[OWN * (2 * j + i) : OWN * (2 * j + i) + OWN]
                at_a = fa_w["x"] * i + fa_w["zl"] * j + fa_w["zh"] * h
                at_b = fb_w["x"] * i + fb_w["zl"] * j + fb_w["zh"] * h
                a.dout_t[part(at_a, OWN), part(w, HALF)] = piece[:, :HALF]
                a.gfb[part(at_b, OWN), part(w, HALF)] = piece[:, HALF:]

    loop(4, weights_fc)
    fa.start(0)
    fb.start(0)
    for load in loads_qkv:
        load.start()
    steps(("back", 0))

    @pl.when(d >= 0)
    def _():
        grad_in = back_of(1)
        for k in (1, 0):
            t = blocks_of(1)[k]
            normed, inverse = stats(a.gres[k])
            g_copy(k).wait_recv()
            grad = grad_in[SPAN * k : SPAN * k + SPAN] + a.gin[k].astype(F32)
            wide = a.drow[t].astype(F32)
            branch = (wide + norm_back(grad * a.gain_two[...], normed, inverse)).astype(BF)
            a.gbr[t] = branch
            b_copy(k).start()
            a.acc[0] += jnp.sum(branch.astype(F32), axis=0, keepdims=True)
            a.acc[1] += jnp.sum(wide, axis=0, keepdims=True)
            a.acc[4] += jnp.sum(grad * normed, axis=0, keepdims=True)
            a.acc[5] += jnp.sum(grad, axis=0, keepdims=True)

    steps(("back", 1))

    @pl.when(d >= 0)
    def _():
        out = out_of(1)
        for k in (1, 0):
            o_copy(k).wait_recv()
            g_copy(k).wait_send()
            whole = a.gres[k] + (out[SPAN * k : SPAN * k + SPAN] + a.oin[k].astype(F32)) + a.b_proj[...]
            a.gbuf[k] = whole.astype(BF)
            if k == 1:
                y_far.start()
            else:
                y_own.start()


    def pack(rows, vectors):
        pieces = [v[:, 128 * i : 128 * i + 128] for v in vectors for i in range(v.shape[1] // 128)]
        pieces += [jnp.zeros((1, 128), F32)] * (rows - len(pieces))
        return jnp.concatenate(pieces, axis=0)

    a.early[0] = jnp.zeros((EARLY, 128), F32)
    a.early[0, :24, :] = pack(24, [a.acc[n] for n in (0, 1, 4, 5)])
    a.early[0, pl.ds(pl.multiple_of(24 + 16 * c, 8), 16), :] = pack(16, [a.acc_bfc[...]])
    ve.start(0)

    b_copy(0).wait_recv()
    b_copy(1).wait_recv()

    def branch_block(t):
        rows = pl.ds(mul(t, SPAN), SPAN)
        grad = nt(a.wout[pl.ds(half_c, HALF), :], a.gbr[t])
        for p in range(3):
            parts = []
            for e in range(2):
                head = 2 * p + e
                at = slice(HEAD * head, HEAD * head + HEAD)
                inverse = a.linv[head, :, rows]
                piece = grad[at].astype(BF).astype(F32)
                a.delta[head, :, rows] = inverse * jnp.sum(
                    piece * a.o_t[at, rows].astype(F32), axis=0, keepdims=True
                )
                parts.append(piece * inverse)
            scaled = jnp.concatenate(parts, axis=0).astype(BF)
            a.hid[rows, 3 * HALF + 128 * p : 3 * HALF + 128 * p + 128] = scaled.T

    loop(4, branch_block)

    steps("branch")
    for n in range(2):
        lhs = a.o_t[2 * OWN * n : 2 * OWN * n + 2 * OWN, :]
        grad = nn(lhs[:, :SPAN], a.gbr[0])
        for t in range(1, BLOCKS):
            grad += nn(lhs[:, SPAN * t : SPAN * t + SPAN], a.gbr[t])
        grad = grad.astype(BF)
        for i in range(2):
            for w in range(2):
                at = OWN * (wo_w["zl"] * n + wo_w["x"] * i + wo_w["y"] * w)
                a.wout[at : at + OWN, :HALF] = grad[OWN * i : OWN * i + OWN, HALF * w : HALF * w + HALF]
    wo.start(0)

    def between(p, i):
        for value in range(3):
            if plan["pair", value, i]:

                @pl.when(p == value)
                def _():
                    steps(("pair", value, i))

    def backward_pair(p):
        cols = pl.ds(mul(p, 128), 128)
        do_cols = pl.ds(pl.multiple_of(3 * HALF + 128 * p, 128), 128)
        a.k_t[...] = a.kn[:, cols].T
        for i in reversed(range(BLOCKS)):
            rows = slice(SPAN * i, SPAN * i + SPAN)
            keys_n = SPAN * (i + 1)
            pair = a.qn[rows, cols]
            do_pair = a.hid[rows, do_cols]

            def grad_scores(e):
                head = 2 * p + e
                mine = (lane >= HEAD * e) & (lane < HEAD * e + HEAD)
                delta = a.delta[head, :, rows]
                product = nt(a.vn[:keys_n, cols], jnp.where(mine, do_pair, jnp.zeros_like(do_pair)))
                for j in range(i + 1):
                    at = base(i) + SPAN * j
                    keys = slice(SPAN * j, SPAN * j + SPAN)
                    weights = a.probs[head, at : at + SPAN, :].astype(F32)
                    low = (weights * (product[keys] - delta)).astype(BF)
                    a.mix[e, keys, :SPAN] = low

            def grad_query(e):
                low = a.mix[e, :keys_n, :SPAN]
                feats = pl.ds(mul(e, HEAD), HEAD)
                a.dq_t[feats, :] = nn(a.k_t[feats, :keys_n], low) * 0.125

            loop(2, grad_scores)
            loop(2, grad_query)
            a.hid[rows, cols] = a.dq_t[...].T.astype(BF)
            masks = [lane < HEAD, lane >= HEAD]
            query_both = jnp.concatenate([jnp.where(m, pair, jnp.zeros_like(pair)) for m in masks], axis=0)
            grad_both = jnp.concatenate([jnp.where(m, do_pair, jnp.zeros_like(pair)) for m in masks], axis=0)
            keys = slice(0, keys_n)
            at = base(i)
            scores = jnp.concatenate([a.mix[n, keys, :SPAN] for n in range(2)], axis=1)
            weights = jnp.concatenate(
                [a.probs[2 * p, at : at + keys_n, :], a.probs[2 * p + 1, at : at + keys_n, :]], axis=1
            )
            part_k = nn(scores, query_both)
            part_v = nn(weights, grad_both)
            if i == BLOCKS - 1:
                a.dk[...] = part_k
                a.dv[...] = part_v
            else:
                a.dk[keys, :] += part_k
                a.dv[keys, :] += part_v
            between(p, i)
        at_k = pl.ds(pl.multiple_of(HALF + 128 * p, 128), 128)
        at_v = pl.ds(pl.multiple_of(2 * HALF + 128 * p, 128), 128)
        low_k, low_v = a.dk[...].astype(BF), a.dv[...].astype(BF)
        a.hid[:, at_k] = low_k
        a.hid[:, at_v] = low_v

        @pl.when(p >= 0)
        def _():
            both = jnp.concatenate([a.hid[:, cols], a.hid[:, at_k], a.hid[:, at_v]], axis=1)
            ones = jnp.ones((16, SEQ), BF)
            grad = nn(jnp.concatenate([a.ain_t[...], ones], axis=0), both)
            a.acc_qv[0, :, cols] = grad[D : D + 1, :128]
            a.acc_qv[1, :, cols] = grad[D : D + 1, SPAN:]
            grad = grad.astype(BF)
            for h in range(2):
                for j in range(2):
                    for i in range(2):
                        at = (4 * h + 2 * j + i) * OWN
                        to = q_w["zh"] * h + q_w["zl"] * j + q_w["x"] * i
                        a.gpre[OWN * to : OWN * to + OWN, part(p, HALF)] = grad[at : at + OWN]

        for n, (pair, _, _) in enumerate(Q_CHAINS):

            @pl.when(p == pair)
            def _():
                qs[n][0].start(0)

        between(p, -1)

    for p in range(3):
        mix_copy(p).wait_send()
    loop(3, backward_pair)

    a_first = numbers(2)
    for load in loads_qkv:
        load.wait()

    def a_copy(s):
        return remote(a.obuf.at[s], a.oin.at[s], a_first + s, to_core)

    x_far = remote(a.gbuf.at[1], a.gx_out.at[y], numbers(1), to_y)
    x_own = pltpu.make_async_copy(a.gbuf.at[0], a.gx_out.at[y], a.local.at[11])

    def input_pair(g):
        ts = blocks_of(g)
        spans = spans_of(ts)
        part_in = nt(stack_rows(a.hid, spans, slice(0, 3 * HALF)), a.wqkv[...])
        for k in (1, 0):
            half = slice(SPAN * k, SPAN * k + SPAN)
            if g == 0:
                a.obuf[k] = part_in[half].astype(BF)
                a_copy(k).start()
                continue
            normed, inverse = stats(a.xrow[ts[k]].astype(F32))
            a_copy(k).wait_recv()
            grad = part_in[half] + a.oin[k].astype(F32)
            total = a.gbr[ts[k]].astype(F32) + norm_back(grad * a.gain_one[...], normed, inverse)
            a.gbuf[k] = total.astype(BF)
            if k == 1:
                x_far.start()
            else:
                x_own.start()
            a.acc[2] += jnp.sum(grad * normed, axis=0, keepdims=True)
            a.acc[3] += jnp.sum(grad, axis=0, keepdims=True)

    y_far.wait()
    y_own.wait()
    for k in range(2):
        o_copy(k).wait_send()

    for g in range(2):
        input_pair(g)
        steps(("input", g))

    share, half_dp = D // dp, dp // 2
    for e in range(dp):
        mine = (c == e // half_dp).astype(F32)
        at, at_half = share * e, share * (e % half_dp)
        rows = [a.acc[2, :, at : at + share], a.acc[3, :, at : at + share]]
        rows += [a.acc_qv[n, :, at_half : at_half + share] * mine for n in range(2)]
        tile = jnp.concatenate(rows + [jnp.zeros((4, share), F32)], axis=0)
        a.late[e] = jnp.concatenate([tile, jnp.zeros((8, 128 - share), F32)], axis=1)
    for copy in late_groups():
        copy.start()
    steps("last")

    for n, device in enumerate(extra):
        outs = (
            (a.gpj_out, a.xs_pj, a.xr_pj),
            (a.gfc_out, a.xs_fc, a.xr_fc),
            (a.gwo_out, a.xs_wo, a.xr_wo),
        )
        copies = []
        for m, (out, sent, came) in enumerate(outs):
            sent[0] = out[...].astype(BF)
            copies.append((out, sent, came, m))
        a.xs_q[0] = a.gq_out[c].astype(BF)
        copies.append((a.gq_out.at[c], a.xs_q, a.xr_q, 3))
        started = []
        for out, sent, came, m in copies:
            copy = pltpu.make_async_remote_copy(
                src_ref=sent.at[0],
                dst_ref=came.at[n],
                send_sem=a.xsend.at[n, m],
                recv_sem=a.xrecv.at[n, m],
                device_id=device,
                device_id_type=MESH,
            )
            copy.start()
            started.append(copy)
        for (out, sent, came, m), copy in zip(copies, started):
            copy.wait()
            out[...] = (sent[0].astype(F32) + came[n].astype(F32)).astype(out.dtype)
    if extra:
        a.xs_q[0] = a.gq_out[c]
        copy = remote(a.xs_q.at[0], a.xc_q, numbers(1), to_core)
        copy.start()
        copy.wait()
        a.gq_out[other] = a.xc_q[...]
    a.early_out[...] = a.early[5 + len(extra)]

    for copy in pending:
        copy.wait_send()
    for chain in chains.values():
        chain.sent()
    for s in range(2):
        a_copy(s).wait_send()
    b_copy(0).wait_send()
    b_copy(1).wait_send()
    for copy in (x_far, x_own):
        copy.wait()
    for copy in late_groups() + late_row():
        copy.wait_send()
    assert count[0] <= 120


def finish_kernel(dp, *refs):
    y_in, gx, gq, gwo, gfc, gpj, early, late = refs[:8]
    (y_out, gx_out, gq_out, bq_out, bv_out, gwo_out, bo_out, gfc_out, bf_out, gpj_out) = refs[8:18]
    rest = refs[18:]
    d = lax.axis_index("dp")
    b = lax.axis_index("blk")
    y, c = lax.div(b, 2), lax.rem(b, 2)
    subs = dp // 8
    sub = lax.rem(d, subs)
    rows = D // dp

    def rows_of(v):
        out = v[:rows]
        for n in range(1, subs):
            out = jnp.where(sub == n, v[rows * n : rows * n + rows], out)
        return out

    y_out[...] = y_in[...]
    gx_out[...] = gx[...].astype(F32)

    @pl.when(pl.program_id(0) == 0)
    def _():
        query = [jnp.concatenate([gq[n, p, :, :128] for p in range(3)], axis=1) for n in range(2)]
        key = [jnp.concatenate([gq[n, p, :, 128:256] for p in range(3)], axis=1) for n in range(2)]
        value = [jnp.concatenate([gq[n, p, :, 256:] for p in range(3)], axis=1) for n in range(2)]
        first = jnp.concatenate([query[0], query[1], key[0]], axis=1)
        second = jnp.concatenate([key[1], value[0], value[1]], axis=1)
        full = jnp.where(y == 0, first, second)
        columns = 3 * D // BLOCKS
        full = full.astype(F32)
        gq_out[...] = rows_of(jnp.where(c == 0, full[:, :columns], full[:, columns:]))
        columns = D // BLOCKS
        gwo_out[...] = rows_of(jnp.where(c == 0, gwo[:, :columns], gwo[:, columns:]))
        gfc_out[...] = rows_of(gfc[...])
        cols_ff = 2 * FF // dp
        out = gpj[:, :cols_ff]
        for n in range(1, subs):
            out = jnp.where(sub == n, gpj[:, cols_ff * n : cols_ff * n + cols_ff], out)
        gpj_out[...] = out

        def line(vec, first_row, n):
            return [vec[first_row + i : first_row + i + 1, :] for i in range(n)]

        def put(out, pieces):
            whole = jnp.concatenate(pieces, axis=1)
            size = whole.shape[1]
            n = size // dp
            turned = pltpu.roll(jnp.broadcast_to(whole, (8, size)), lax.rem(size - d * n, size), 1)
            out[...] = turned[0, :n]

        bq_out[...] = late[2, :rows]
        bv_out[...] = late[3, :rows]
        put(bo_out, line(early, 0, 6))
        put(bf_out, line(early, 24, 6) + line(early, 40, 6) + line(early, 30, 6) + line(early, 46, 6))
        for out, first_row in zip((rest[0], rest[3], rest[4]), (6, 12, 18)):
            put(out, line(early, first_row, 6))
        rest[1][...] = late[0, :rows]
        rest[2][...] = late[1, :rows]


def body(dp, layer_input, lengths, w_qkv, b_query, b_value, w_out, b_out, w_fc, b_fc, w_proj, b_proj, *more):
    d_out = more[4]
    vectors = (b_query, b_value, b_out, b_proj) + more[:4] + (b_fc,)
    args = (layer_input, lengths, w_qkv, w_out, w_fc, w_proj, d_out) + vectors
    shapes = scratch(dp)
    spaces = [pl.ANY, pltpu.SMEM] + [pl.ANY] * 5 + [pltpu.VMEM] * len(VECTORS)
    in_specs = [pl.BlockSpec(memory_space=space) for space in spaces]
    out_shape = (
        jax.ShapeDtypeStruct((2, SPAN, D), BF),
        jax.ShapeDtypeStruct((2, SPAN, D), BF),
        jax.ShapeDtypeStruct((2, 3, OWN, HALF), BF),
        jax.ShapeDtypeStruct((OWN, HALF), F32),
        jax.ShapeDtypeStruct((OWN, D), F32),
        jax.ShapeDtypeStruct((HALF // 2, HALF), F32),
        jax.ShapeDtypeStruct((EARLY, 128), F32),
        jax.ShapeDtypeStruct((8, 128), F32),
    )
    out_specs = [pl.BlockSpec(memory_space=pl.ANY)] * 2 + [pl.BlockSpec(memory_space=pltpu.VMEM)] * 6
    outs = pl.pallas_call(
        functools.partial(kernel, dp, INPUTS + OUTPUTS + tuple(shapes)),
        out_shape=out_shape,
        in_specs=in_specs,
        out_specs=out_specs,
        scratch_shapes=list(shapes.values()),
        compiler_params=pltpu.CompilerParams(
            collective_id=0, has_side_effects=True, vmem_limit_bytes=63 * 1024 * 1024
        ),
    )(*args)
    rows = D // dp
    line = jax.ShapeDtypeStruct((rows,), F32)
    out_shape = (
        jax.ShapeDtypeStruct((2, SPAN, D), BF),
        jax.ShapeDtypeStruct((2, SPAN, D), F32),
        jax.ShapeDtypeStruct((rows, 3 * D // BLOCKS), F32),
        line,
        line,
        jax.ShapeDtypeStruct((rows, D // BLOCKS), F32),
        line,
        jax.ShapeDtypeStruct((rows, D), F32),
        jax.ShapeDtypeStruct((2 * FF // dp,), F32),
        jax.ShapeDtypeStruct((D // BLOCKS, 2 * FF // dp), F32),
    ) + (line,) * 5

    def specs(arrays):
        by_row = pl.BlockSpec((1, SPAN, D), lambda n: (n, 0, 0))
        return [by_row, by_row] + [
            pl.BlockSpec(v.shape, lambda n, rank=len(v.shape): (0,) * rank) for v in arrays[2:]
        ]

    done = pl.pallas_call(
        functools.partial(finish_kernel, dp),
        grid=(2,),
        out_shape=out_shape,
        in_specs=specs(outs),
        out_specs=specs(out_shape),
        compiler_params=pltpu.CompilerParams(vmem_limit_bytes=63 * 1024 * 1024),
    )(*outs)
    return tuple(done[:9]) + (done[9].T,) + tuple(done[10:])


def solution(mesh):
    rows = P("dp", "blk", None)
    grid = P("dp", "blk")
    line = P("dp")
    in_specs = (rows, P("dp", None)) + (P(),) * 13 + (rows,)
    out_specs = (rows, rows, grid, line, line, grid, line, grid, line, grid) + (line,) * 5
    dp = mesh.shape["dp"]
    return jax.shard_map(
        functools.partial(body, dp),
        mesh=mesh,
        in_specs=in_specs,
        out_specs=out_specs,
        check_vma=False,
    )
```

```python
import functools
import itertools

import jax
import jax.numpy as jnp
from jax import lax
from jax.experimental import pallas as pl
from jax.experimental.pallas import tpu as pltpu
from jax.sharding import PartitionSpec as P

HEADS = 12
HEAD = 64

ln_epsilon = 1e-05
gelu_factor = 0.7978845608028654
big_negative = -1e30

BF = jnp.bfloat16
F32 = jnp.float32
MESH = pl.DeviceIdType.MESH

SPAN = 256
BLOCKS = 4
SEQ = SPAN * BLOCKS
D = 768
HALF = D // 2
FF = 1536
CHUNK = 512
OWN = 96

PA_ORDER = ("x", "zh", "y")
PB_ORDER = ("zh", "y", "x")
FA_ORDER = ("zl", "y", "x", "zh")
FB_ORDER = ("y", "zl", "x", "zh")
WO_ORDER = ("y", "zl", "x")
Q_ORDER = ("x", "zl", "zh")
Q_CHAINS = ((0, 0, 3), (1, 0, 3), (2, 0, 3))


PLACES = (
    [("back", n) for n in range(2)]
    + ["branch"]
    + [("pair", p, i) for p in range(3) for i in (3, 2, 1, 0, -1)]
    + [("input", n) for n in range(2)]
    + ["last"]
)
STEPS = {
    "branch": ["pa"],
    ("pair", 0, -1): ["ve"],
    ("pair", 1, 2): ["ve"],
    ("pair", 1, 1): ["pb", "fa"],
    ("pair", 1, -1): ["fb", "q0"],
    ("pair", 2, 2): ["pa"],
    ("pair", 2, -1): ["wo", "q1", "q0"],
    ("input", 1): ["fb"],
    "last": (
        ["q2", "q0", "pa", "pa", "vl", "fb", "wo", "pb", "q1", "fa", "vl", "q0", "q0", "wo", "q2", "pa", "wo"]
        + ["pb", "fa", "fb", "pb", "q1", "pb", "wo", "fa", "sent", "q2", "q1", "q1"]
    ),
}


def numbered():
    seen, out = {}, {}
    for place in PLACES:
        names = list(STEPS.get(place, ()))
        out[place] = []
        for name in names:
            out[place].append((name, seen.get(name, 0)))
            seen[name] = seen.get(name, 0) + 1
    return out


def proj_lands(order):
    rows, halves, shapes = D, 2, []
    for axis in order:
        if axis == "zh":
            halves = 1
        else:
            rows //= 2
        shapes.append((halves, rows, HALF))
    return shapes + [(2, OWN, HALF), (OWN, HALF)]


def fc_lands(order):
    rows, cols, shapes = D, D, []
    for axis in order:
        if axis == "y":
            cols //= 2
        else:
            rows //= 2
        shapes.append((rows, cols))
    return shapes


def row_lands(order, cols):
    return [(D >> (n + 1), cols) for n in range(len(order))]


def row_weights(order, last=1):
    return {axis: last << (len(order) - 1 - n) for n, axis in enumerate(order)}


def stats(v):
    centre = jnp.mean(v, axis=-1, keepdims=True)
    centered = v - centre
    inverse = lax.rsqrt(jnp.mean(centered * centered, axis=-1, keepdims=True) + ln_epsilon)
    return centered * inverse, inverse


def norm_back(grad_norm, normed, inverse):
    first = jnp.mean(grad_norm, axis=-1, keepdims=True)
    second = jnp.mean(grad_norm * normed, axis=-1, keepdims=True)
    return inverse * (grad_norm - first - normed * second)


def nn(a, b):
    return jnp.dot(a, b, preferred_element_type=F32)


def nt(a, b):
    return lax.dot_general(a, b, (((1,), (1,)), ((), ())), preferred_element_type=F32)


def mul(i, n):
    return pl.multiple_of(i * n, n)


def loop(n, body):
    def step(i, carry):
        body(i)
        return carry

    lax.fori_loop(0, n, step, 0)


def gelu_both(v):
    square = v * v
    inner = jnp.tanh(v * (gelu_factor + 0.044715 * gelu_factor * square))
    half = 0.5 + 0.5 * inner
    value = v * half
    return value, half + value * ((1.0 - inner) * (gelu_factor + 3.0 * 0.044715 * gelu_factor * square))


def top_of(v):
    while v.shape[0] > 8:
        half = v.shape[0] // 2
        v = jnp.maximum(v[:half], v[half:])
    return v


def base(i):
    return SPAN * (i * (i + 1) // 2)


def scratch(dp):
    extras = max(0, dp.bit_length() - 4)
    vm = pltpu.VMEM
    shapes = dict(
        xrow=vm((BLOCKS, SPAN, D), BF),
        drow=vm((BLOCKS, SPAN, D), BF),
        wqkv=vm((D, 3 * HALF), BF),
        wout=vm((D, D), BF),
        wfc=vm((D, FF), BF),
        wproj=vm((FF, D), BF),
        bfc=vm((1, FF), F32),
        ain_t=vm((D, SEQ), BF),
        qn=vm((SEQ, HALF), BF),
        kn=vm((SEQ, HALF), BF),
        vn=vm((SEQ, HALF), BF),
        k_t=vm((128, SEQ), BF),
        v_t=vm((6, HEAD + 16, SEQ), BF),
        start=vm((BLOCKS, 1, SPAN), jnp.int32),
        probs=vm((6, base(4), SPAN), BF),
        linv=vm((6, 1, SEQ), F32),
        delta=vm((6, 1, SEQ), F32),
        o_t=vm((HALF, SEQ), BF),
        mix=vm((2, SEQ, HALF), BF),
        gpj=vm((D, FF), BF),
        gfb=vm((D, D), BF),
        vectors=vm((1, 8 * D + 2 * FF), F32),
        dout_t=vm((D, SEQ), BF),
        hid=vm((SEQ, FF), BF),
        gpre=vm((SEQ, FF), BF),
        obuf=vm((2, SPAN, D), BF),
        oin=vm((2, SPAN, D), BF),
        gbuf=vm((2, SPAN, D), BF),
        gin=vm((2, SPAN, D), BF),
        gres=vm((2, SPAN, D), F32),
        gbr=vm((BLOCKS, SPAN, D), BF),
        dk=vm((SEQ, 128), F32),
        dv=vm((SEQ, 128), F32),
        acc_bfc=vm((1, FF), F32),
        acc_qv=vm((2, 1, HALF), F32),
        acc=vm((6, 1, D), F32),
    )
    for name in ("early", "late"):
        shapes.update(
            {
                name: vm((dp, 8, 128), F32),
                name + "_r": vm((dp, 8, 128), F32),
                name + "_s": vm((8, 128), F32),
                name + "_q": vm((3, 8, 128), F32),
                name + "_send": pltpu.SemaphoreType.DMA((dp + 3,)),
                name + "_recv": pltpu.SemaphoreType.DMA((dp + 3,)),
            }
        )
    shapes.update(
        local=pltpu.SemaphoreType.DMA((16,)),
        send=pltpu.SemaphoreType.DMA((120,)),
        recv=pltpu.SemaphoreType.DMA((120,)),
    )
    lands = dict(
        pa=proj_lands(PA_ORDER),
        pb=proj_lands(PB_ORDER),
        fa=fc_lands(FA_ORDER),
        fb=fc_lands(FB_ORDER),
        wo=row_lands(WO_ORDER, HALF) + [(2, OWN, HALF), (OWN, HALF)],
    )
    for n, (_, _, units) in enumerate(Q_CHAINS):
        cols = 128 * units
        if n < 2:
            lands[f"q{n}"] = row_lands(Q_ORDER, cols) + [(OWN, cols)] * 3
        else:
            lands[f"q{n}"] = [(4 * OWN, cols), (3, OWN, cols), (3, OWN, cols)]
    for name, sizes in lands.items():
        for n, size in enumerate(sizes):
            shapes[f"{name}_{n}"] = vm(size, BF)
    if extras:
        shapes.update(
            xs_pj=vm((1, HALF // 2, HALF), BF),
            xr_pj=vm((extras, HALF // 2, HALF), BF),
            xs_fc=vm((1, OWN, D), BF),
            xr_fc=vm((extras, OWN, D), BF),
            xs_wo=vm((1, OWN, HALF), BF),
            xr_wo=vm((extras, OWN, HALF), BF),
            xs_q=vm((1, 3, OWN, HALF), BF),
            xr_q=vm((extras, 3, OWN, HALF), BF),
            xc_q=vm((3, OWN, HALF), BF),
            xsend=pltpu.SemaphoreType.DMA((extras, 4)),
            xrecv=pltpu.SemaphoreType.DMA((extras, 4)),
        )
    return shapes


VECTORS = ("b_query", "b_value", "b_out", "b_proj", "gain_one", "shift_one", "gain_two", "shift_two", "b_fc")
INPUTS = ("x_in", "lengths", "w_qkv", "w_out", "w_fc", "w_proj", "d_in") + tuple(n + "_in" for n in VECTORS)
OUTPUTS = ("y_out", "gx_out", "gq_out", "gwo_out", "gfc_out", "gpj_out", "early_out", "late_out")


def kernel(dp, names, *refs):
    r = dict(zip(names, refs))
    a = type("Refs", (), r)
    for n, name in enumerate(VECTORS):
        size = 2 * FF if name == "b_fc" else D
        a.vectors[:, D * n : D * n + size] = r[name + "_in"][...].reshape(1, size)
        setattr(a, name, a.vectors.at[:, D * n : D * n + size])
    d = lax.axis_index("dp")
    b = lax.axis_index("blk")
    y = lax.div(b, 2)
    c = lax.rem(b, 2)
    other = 1 - c

    def bit(weight):
        return lax.rem(lax.div(d, weight), 2)

    def across(weight):
        return (d + weight * (1 - 2 * bit(weight)), b)

    t2, t1, t0 = bit(dp // 2), bit(dp // 4), bit(dp // 8)
    to_core = (d, 2 * y + other)
    to_y = (d, 2 * (1 - y) + c)
    to2, to1, to0 = across(dp // 2), across(dp // 4), across(dp // 8)
    to21 = (to2[0] + to1[0] - d, b)
    to_diagonal = (d, 2 * (1 - y) + other)
    groups = [(lax.rem(d + n, dp), b) for n in range(1, dp)]
    extra = []
    weight = dp // 16
    while weight >= 1:
        extra.append(across(weight))
        weight //= 2

    count = [0]

    def numbers(n):
        count[0] += n
        return count[0] - n

    def remote(src, dst, number, device):
        return pltpu.make_async_remote_copy(
            src_ref=src,
            dst_ref=dst,
            send_sem=a.send.at[number],
            recv_sem=a.recv.at[number],
            device_id=device,
            device_id_type=MESH,
        )

    pending = []

    def post(src, dst, device):
        copy = remote(src, dst, numbers(1), device)
        copy.start()
        pending.append(copy)
        return copy

    barrier = pltpu.get_barrier_semaphore()
    partners = [to_core, to_y, to_diagonal] + groups
    for device in partners:
        pl.semaphore_signal(barrier, inc=1, device_id=device, device_id_type=MESH)
    pl.semaphore_wait(barrier, len(partners))

    far = 2 * (1 - y) + c
    near_p = 2 * y + other
    far_p = 2 * (1 - y) + other
    x_y = post(a.x_in.at[1 - y], a.xrow.at[b], to_y)
    x_c = post(a.x_in.at[y], a.xrow.at[b], to_core)
    x_l = pltpu.make_async_copy(a.x_in.at[y], a.xrow.at[b], a.local.at[0])
    x_l.start()
    half_c = mul(c, HALF)
    loads_qkv = []
    for u in range(3):
        loads_qkv.append(
            pltpu.make_async_copy(
                a.w_qkv.at[:, pl.ds(pl.multiple_of(D * u + c * HALF, 128), HALF)],
                a.wqkv.at[:, pl.ds(HALF * u, HALF)],
                a.local.at[1 + u],
            )
        )
    loads_mlp = [pltpu.make_async_copy(a.w_out, a.wout, a.local.at[4])]
    for h in range(2):
        ff_at = pl.ds(pl.multiple_of(h * FF + c * D, 128), D)
        loads_mlp.append(
            pltpu.make_async_copy(a.w_fc.at[:, ff_at], a.wfc.at[:, pl.ds(h * D, D)], a.local.at[5 + h])
        )
        loads_mlp.append(
            pltpu.make_async_copy(a.w_proj.at[ff_at], a.wproj.at[pl.ds(h * D, D)], a.local.at[7 + h])
        )
        a.bfc[:, h * D : h * D + D] = a.b_fc[:, ff_at]
    d_l = pltpu.make_async_copy(a.d_in.at[y], a.drow.at[b], a.local.at[9])
    for load in loads_qkv + [d_l] + loads_mlp:
        load.start()
    d_y = remote(a.d_in.at[1 - y], a.drow.at[b], numbers(1), to_y)
    pending.append(d_y)
    d_c = post(a.d_in.at[y], a.drow.at[b], to_core)

    position = lax.broadcasted_iota(jnp.int32, (1, SPAN), 1)
    for i in range(BLOCKS):
        begin = jnp.zeros((1, SPAN), jnp.int32)
        total = jnp.int32(0)
        for j in range(8):
            total = total + a.lengths[y, j]
            begin = jnp.where(position + SPAN * i >= total, total, begin)
        a.start[i] = begin
    a.acc[...] = jnp.zeros_like(a.acc)
    a.v_t[:, HEAD:, :] = jnp.ones((6, 16, SEQ), BF)

    for load in loads_qkv:
        load.wait()
    bias_q = a.b_query[:, pl.ds(half_c, HALF)]
    bias_v = a.b_value[:, pl.ds(half_c, HALF)]

    def project(t):
        rows = pl.ds(mul(t, SPAN), SPAN)
        normed, _ = stats(a.xrow[t].astype(F32))
        low = (normed * a.gain_one[...] + a.shift_one[...]).astype(BF)
        out = nn(low, a.wqkv[...])
        a.qn[rows, :] = ((out[:, :HALF] + bias_q).astype(BF).astype(F32) * 0.125).astype(BF)
        values = (out[:, 2 * HALF :] + bias_v).astype(BF)
        turned = values.T
        a.kn[rows, :] = out[:, HALF : 2 * HALF].astype(BF)
        a.vn[rows, :] = values
        for h in range(6):
            a.v_t[h, :HEAD, rows] = turned[HEAD * h : HEAD * h + HEAD]

    def turn(t):
        rows = pl.ds(mul(t, SPAN), SPAN)
        normed, _ = stats(a.xrow[t].astype(F32))
        a.ain_t[:, rows] = (normed * a.gain_one[...] + a.shift_one[...]).astype(BF).T

    def turn_d(t):
        a.dout_t[:, pl.ds(mul(t, SPAN), SPAN)] = a.drow[t].T

    def stack(ref, ts):
        return jnp.concatenate([ref[t] for t in ts], axis=0)

    def stack_rows(ref, spans, cols=slice(None)):
        return jnp.concatenate([ref[rows, cols] for rows in spans], axis=0)

    def spans_of(ts):
        return [pl.ds(mul(t, SPAN), SPAN) for t in ts]

    def grad_hidden(ts, slopes):
        spans = spans_of(ts)
        top = stack(a.drow, ts)
        for f in range(0, FF, CHUNK):
            here = slice(f, f + CHUNK)
            grad = nt(top, a.wproj[here, :])
            if slopes:
                grad = grad * stack_rows(a.gpre, spans, here).astype(F32)
            grad = grad.astype(BF)
            for k, rows in enumerate(spans):
                a.gpre[rows, here] = grad[SPAN * k : SPAN * k + SPAN]

    fwd_x = remote(a.xrow.at[far], a.xrow.at[far], numbers(1), to_core)
    fwd_d = remote(a.drow.at[far], a.drow.at[far], numbers(1), to_core)
    pending += [fwd_x, fwd_d]

    def arrive(s):
        @pl.when(s == 0)
        def _():
            x_l.wait()

        @pl.when(s == 1)
        def _():
            x_c.wait_recv()

        @pl.when(s == 2)
        def _():
            x_y.wait_recv()
            fwd_x.start()
            d_y.start()

        @pl.when(s == 3)
        def _():
            fwd_x.wait_recv()

        far_s = lax.div(s, 2)
        core_s = lax.rem(s, 2)
        t = 2 * (y + far_s * (1 - 2 * y)) + c + core_s * (1 - 2 * c)
        project(t)

        @pl.when(s == 0)
        def _():
            d_l.wait()

        @pl.when(s == 1)
        def _():
            d_c.wait_recv()

            for load in loads_mlp:
                load.wait()

        @pl.when(s < 2)
        def _():
            turn(t)
            turn_d(t)

        @pl.when(s == 1)
        def _():
            grad_hidden((b, near_p), False)

    loop(4, arrive)

    lane = lax.broadcasted_iota(jnp.int32, (1, 128), 1)
    key_index = lax.broadcasted_iota(jnp.int32, (SPAN, SPAN), 0)
    query_index = lax.broadcasted_iota(jnp.int32, (SPAN, SPAN), 1)
    mix_first = numbers(3)

    def mix_copy(p):
        here = a.mix.at[c, :, pl.ds(mul(p, 128), 128)]
        return remote(here, here, mix_first + p, to_core)

    def forward_pair(p):
        cols = pl.ds(mul(p, 128), 128)
        for i in range(BLOCKS):
            rows = slice(SPAN * i, SPAN * i + SPAN)
            keys_n = SPAN * (i + 1)
            pair = a.qn[rows, cols]
            begin = a.start[i]
            for e in range(2):
                head = 2 * p + e
                query = jnp.where(lane // HEAD == e, pair, jnp.zeros_like(pair))
                scores, tops = [], []
                product = nt(a.kn[:keys_n, cols], query)
                for j in range(i + 1):
                    s = product[SPAN * j : SPAN * j + SPAN]
                    ok = key_index + SPAN * j >= begin
                    if j == i:
                        ok = ok & (key_index <= query_index)
                    s = jnp.where(ok, s, big_negative)
                    scores.append(s)
                    tops.append(top_of(s))
                top = tops[0]
                for here in tops[1:]:
                    top = jnp.maximum(top, here)
                top = jnp.max(top, axis=0, keepdims=True)
                for j in range(i + 1):
                    at = base(i) + SPAN * j
                    a.probs[head, at : at + SPAN, :] = jnp.exp(scores[j] - top).astype(BF)

        @pl.when(p >= 0)
        def _():
            for e, i in itertools.product(range(2), range(BLOCKS)):
                head = 2 * p + e
                feats = pl.ds(mul(head, HEAD), HEAD)
                rows = slice(SPAN * i, SPAN * i + SPAN)
                keys_n = SPAN * (i + 1)
                out = nn(a.v_t[head, :, :keys_n], a.probs[head, base(i) : base(i) + keys_n, :])
                inverse = 1.0 / out[HEAD : HEAD + 1]
                a.linv[head, :, rows] = inverse
                a.o_t[feats, rows] = (out[:HEAD] * inverse).astype(BF)

        a.mix[c, :, cols] = a.o_t[pl.ds(mul(p, 128), 128), :].T
        mix_copy(p).start()

        @pl.when(p == 2)
        def _():
            d_y.wait_recv()
            fwd_d.start()

    loop(3, forward_pair)
    turn(far)
    turn(far_p)

    for p in range(3):
        mix_copy(p).wait_recv()

    o_first, g_first, b_first = numbers(2), numbers(2), numbers(2)

    def o_copy(s):
        return remote(a.obuf.at[s], a.oin.at[s], o_first + s, to_core)

    def g_copy(s):
        return remote(a.gbuf.at[s], a.gin.at[s], g_first + s, to_core)

    def b_copy(k):
        t = far if k else b
        return remote(a.gbr.at[t], a.gbr.at[t], b_first + k, to_core)

    y_far = remote(a.gbuf.at[1], a.y_out.at[y], numbers(1), to_y)
    y_own = pltpu.make_async_copy(a.gbuf.at[0], a.y_out.at[y], a.local.at[10])

    def blocks_of(g):
        core = other + g * (2 * c - 1)
        return 2 * y + core, 2 * (1 - y) + core

    def layer_pair(g):
        ts = blocks_of(g)
        spans = spans_of(ts)
        mixed = jnp.concatenate([stack_rows(a.mix.at[n], spans) for n in range(2)], axis=1)
        residual = stack(a.xrow, ts).astype(F32) + nn(mixed, a.wout[...]) + a.b_out[...]
        normed, _ = stats(residual)
        low = (normed * a.gain_two[...] + a.shift_two[...]).astype(BF)
        for k, rows in enumerate(spans):
            a.wqkv[:, rows] = low[SPAN * k : SPAN * k + SPAN].T
        for f in range(0, FF, CHUNK):
            here = slice(f, f + CHUNK)
            value, slope = gelu_both(nn(low, a.wfc[:, here]) + a.bfc[:, here])
            value = value.astype(BF)
            a.hid[spans[0], here] = value[:SPAN]
            a.hid[spans[1], here] = value[SPAN:]
            a.gpre[spans[0], here] = (slope[:SPAN] * a.gpre[spans[0], here].astype(F32)).astype(BF)
            a.gpre[spans[1], here] = slope[SPAN:].astype(BF)

        @pl.when(g == 1)
        def _():
            a.gres[0] = residual[:SPAN]
            a.gres[1] = residual[SPAN:]

    loop(2, layer_pair)
    fwd_d.wait_recv()
    turn_d(far)
    turn_d(far_p)

    def part(first, size, n=1):
        return pl.ds(pl.multiple_of(first * size, size), n * size)

    class Chain:
        def __init__(self, stages):
            self.stages = [one_copy(*stage) if len(stage) == 4 else stage for stage in stages]
            self.first = [numbers(len(stage[0])) for stage in self.stages]

        def copies(self, k):
            pieces, _, device = self.stages[k]
            made = [piece() for piece in pieces]
            return [
                remote(piece[0], piece[1], self.first[k] + n, piece[2] if device is None else device)
                for n, piece in enumerate(made)
            ]

        def start(self, k):
            for copy in self.copies(k):
                copy.start()

        def arrive(self, k):
            for copy in self.copies(k):
                copy.wait_recv()

        def step(self, k):
            self.arrive(k)
            keep = self.stages[k][1]
            if keep is not None:
                keep()
            self.start(k + 1)

        def sent(self):
            for k in range(len(self.stages)):
                for copy in self.copies(k):
                    copy.wait_send()

    def plus(keep, came):
        kept, landed = keep(), came()
        kept[...] = kept[...] + landed[...]

    def one_copy(out, land, keep, device):
        landing = land if callable(land) else lambda: land
        return [lambda: (out(), landing())], (lambda: plus(keep, landing)) if keep else None, device

    axes = dict(x=(t0, to0), zl=(t1, to1), zh=(t2, to2), y=(y, to_y))

    def lands_of(name, n):
        return [r[f"{name}_{k}"] for k in range(n)]

    def proj_chain(name, first, order):
        lands = lands_of(name, 5)
        own, last = lands[3], lands[4]

        def at(block, n, h):
            rows = pl.ds(pl.multiple_of(OWN * block, OWN), OWN * n)
            return a.gpj.at[rows, pl.ds(pl.multiple_of(D * h + first, HALF), HALF)]

        stages = []
        start, width, halves = 0, 8, (0, 1)
        for k, axis in enumerate(order):
            mine, device = axes[axis]
            if axis == "zh":
                pairs = [(start, width, 1 - mine, start, mine)]
                halves = (mine,)
            else:
                width //= 2
                gone, kept = start + (1 - mine) * width, start + mine * width
                pairs = [(gone, width, h, kept, h) for h in halves]
                start = kept
            pieces = [
                lambda p=p, k=k, n=n: (at(p[0], p[1], p[2]), lands[k].at[n]) for n, p in enumerate(pairs)
            ]

            def keep(pairs=pairs, k=k, final=k == len(order) - 1, start=start):
                for n, p in enumerate(pairs):
                    plus(lambda: at(p[3], p[1], p[4]), lambda: lands[k].at[n])
                if final:
                    own[c] = at(start + c, 1, t2)[...]

            stages.append((pieces, keep, device))
        stages.append(([lambda: (at(start + other, 1, t2), own.at[c])], None, to_core))
        stages.append(([lambda: (own.at[1 - t1], last)], None, to1))
        return Chain(stages)

    pa = proj_chain("pa", 0, PA_ORDER)
    pb = proj_chain("pb", HALF, PB_ORDER)

    def fc_chain(name, buf, order):
        lands = lands_of(name, 4)

        def at(block, n, w):
            rows = pl.ds(pl.multiple_of(OWN * block, OWN), OWN * n)
            if w is None:
                return buf.at[rows, pl.ds(0, D)]
            return buf.at[rows, part(w, HALF)]

        stages = []
        start, width, side = 0, 8, None
        for k, axis in enumerate(order):
            mine, device = axes[axis]
            if axis == "y":
                gone, kept = (start, width, 1 - y), (start, width, y)
                side = y
            else:
                width //= 2
                gone, kept = (start + (1 - mine) * width, width, side), (start + mine * width, width, side)
                start = kept[0]
            final = k == len(order) - 1
            stages.append(
                (
                    lambda gone=gone: at(*gone),
                    lands[k],
                    None if final else lambda kept=kept: at(*kept),
                    device,
                )
            )
        return Chain(stages), lambda: at(start, 1, y), lands[-1]

    fa, fa_own, fa_last = fc_chain("fa", a.dout_t, FA_ORDER)
    fb, fb_own, fb_last = fc_chain("fb", a.gfb, FB_ORDER)

    def row_stages(at, order, lands):
        stages = []
        start, width = 0, 8
        for k, axis in enumerate(order):
            mine, device = axes[axis]
            width //= 2
            gone, kept = start + (1 - mine) * width, start + mine * width
            stages.append(
                (
                    lambda gone=gone, width=width: at(gone, width),
                    lands[k],
                    lambda kept=kept, width=width: at(kept, width),
                    device,
                )
            )
            start = kept
        return stages, lambda: at(start, 1)

    wo_lands = lands_of("wo", 5)
    wo_stages, wo_own = row_stages(
        lambda block, n: a.wout.at[pl.ds(pl.multiple_of(OWN * block, OWN), OWN * n), pl.ds(0, HALF)],
        WO_ORDER,
        wo_lands,
    )

    def wo_keep():
        kept = wo_own()
        total = (kept[...].astype(F32) + wo_lands[2][...].astype(F32)).astype(BF)
        kept[...] = total
        wo_lands[3][c] = total

    wo = Chain(
        wo_stages[:2]
        + [
            ([lambda: (wo_stages[2][0](), wo_lands[2])], wo_keep, wo_stages[2][3]),
            (wo_own, lambda: wo_lands[3].at[c], None, to_core),
            (lambda: wo_lands[3].at[1 - t2], wo_lands[4], None, to2),
        ]
    )

    def q_chain(n):
        p, first, units = Q_CHAINS[n]
        cols = slice(HALF * p + 128 * first, HALF * p + 128 * (first + units))

        def at(block, n_blocks):
            return a.gpre.at[pl.ds(pl.multiple_of(OWN * block, OWN), OWN * n_blocks), cols]

        def put(core, value):
            a.gq_out[core, p, :, pl.ds(128 * first, 128 * units)] = value

        if n >= 2:
            came_x, came_z, came = lands_of(f"q{n}", 3)
            start = 4 * t0
            own = lambda: at(start + 2 * t1 + t2, 1)
            around = ((2 * (1 - t1) + t2, to1), (2 * t1 + 1 - t2, to2), (2 * (1 - t1) + 1 - t2, to21))

            def keep_z():
                total = own()[...].astype(F32)
                for m in range(3):
                    total = total + came_z[m].astype(F32)
                own()[...] = total.astype(BF)

            def finish():
                chain.arrive(2)
                put(c, own()[...] + came[0])
                put(other, came[1] + came[2])

            chain = Chain(
                [
                    (lambda: at(4 * (1 - t0), 4), came_x, lambda: at(start, 4), to0),
                    (
                        [
                            lambda m=m, block=block, device=device: (at(start + block, 1), came_z.at[m], device)
                            for m, (block, device) in enumerate(around)
                        ],
                        keep_z,
                        None,
                    ),
                    (
                        [
                            lambda m=m, device=device: (own(), came.at[m], device)
                            for m, device in enumerate((to_y, to_core, to_diagonal))
                        ],
                        None,
                        None,
                    ),
                ]
            )
            return chain, finish
        lands = lands_of(f"q{n}", 6)
        stages, own = row_stages(at, Q_ORDER, lands)

        def keep_y():
            lands[5][...] = own()[...] + lands[3][...]

        def finish():
            chain.arrive(4)
            put(c, lands[5][...])
            put(other, lands[4][...])

        chain = Chain(
            stages + [([lambda: (own(), lands[3])], keep_y, to_y), (lambda: lands[5], lands[4], None, to_core)]
        )
        return chain, finish

    class Spread:
        def __init__(self, name, out):
            self.own, self.came, self.sum, self.row, self.send, self.recv = (
                r[name + end] for end in ("", "_r", "_s", "_q", "_send", "_recv")
            )
            self.out = out

        def copy(self, src, dst, number, device):
            return pltpu.make_async_remote_copy(
                src_ref=src,
                dst_ref=dst,
                send_sem=self.send.at[number],
                recv_sem=self.recv.at[number],
                device_id=device,
                device_id_type=MESH,
            )

        def to_groups(self):
            return [self.copy(self.own.at[to[0]], self.came.at[n + 1], n, to) for n, to in enumerate(groups)]

        def to_row(self):
            row = (to_core, to_y, to_diagonal)
            return [self.copy(self.sum, self.row.at[n], dp - 1 + n, to) for n, to in enumerate(row)]

        def start(self, tiles):
            for e in range(dp):
                pieces = [
                    jnp.concatenate([v, jnp.zeros((1, 128 - v.shape[1]), F32)], axis=1) if v.shape[1] < 128 else v
                    for v in tiles(e)
                ]
                pieces += [jnp.zeros((8 - len(pieces), 128), F32)]
                self.own[e] = jnp.concatenate(pieces, axis=0)
            for copy in self.to_groups():
                copy.start()

        def step(self, k):
            if k == 0:
                for copy in self.to_groups():
                    copy.wait_recv()
                total = self.own[d]
                for n in range(1, dp):
                    total = total + self.came[n]
                self.sum[...] = total
                for copy in self.to_row():
                    copy.start()
            else:
                for copy in self.to_row():
                    copy.wait_recv()
                self.out[...] = self.sum[...] + self.row[0] + self.row[1] + self.row[2]

        def sent(self):
            for copy in self.to_groups() + self.to_row():
                copy.wait_send()

    spread = dict(ve=Spread("early", a.early_out), vl=Spread("late", a.late_out))
    share, share_ff = D // dp, 2 * FF // dp

    def early_tiles(e):
        rows = [a.acc[n, :, share * e : share * e + share] for n in (0, 1, 4, 5)]
        at = share_ff * e
        mine = (c == (at % FF) // D).astype(F32)
        at = at // FF * D + at % D
        for n in range(0, share_ff, 128):
            rows.append(a.acc_bfc[:, at + n : at + min(n + 128, share_ff)] * mine)
        return rows

    def late_tiles(e):
        half_dp = dp // 2
        mine = (c == e // half_dp).astype(F32)
        at, at_half = share * e, share * (e % half_dp)
        rows = [a.acc[n, :, at : at + share] for n in (2, 3)]
        return rows + [a.acc_qv[n, :, at_half : at_half + share] * mine for n in range(2)]

    qs = [q_chain(n) for n in range(len(Q_CHAINS))]

    def finish(chain, out, keep, land):
        chain.arrive(len(chain.stages) - 1)
        out[...] = keep[...].astype(F32) + land[...].astype(F32)

    chains = dict(pa=pa, pb=pb, fa=fa, fb=fb, wo=wo)
    last_steps = dict(
        pa=lambda: finish(pa, a.gpj_out.at[pl.ds(0, OWN)], r["pa_3"].at[t1], r["pa_4"]),
        pb=lambda: finish(pb, a.gpj_out.at[pl.ds(OWN, OWN)], r["pb_3"].at[t1], r["pb_4"]),
        fa=lambda: finish(fa, a.gfc_out.at[:, pl.ds(0, HALF)], fa_own(), fa_last),
        fb=lambda: finish(fb, a.gfc_out.at[:, pl.ds(HALF, HALF)], fb_own(), fb_last),
        wo=lambda: finish(wo, a.gwo_out, wo_lands[3].at[t2], wo_lands[4]),
    )
    for n, name in enumerate(("q0", "q1", "q2")):
        chains[name], last_steps[name] = qs[n]
    plan = numbered()
    assert sum(len(todo) for todo in plan.values()) == 5 + sum(len(chain.stages) for chain in chains.values())

    early_done = [chains[name] for name in ("pa", "pb", "fa", "fb", "wo", "q0")] + list(spread.values())

    def steps(place):
        for name, k in plan[place]:
            if name in spread:
                spread[name].step(k)
            elif name == "sent":
                for each in early_done:
                    each.sent()
            elif k == len(chains[name].stages) - 1:
                last_steps[name]()
            else:
                chains[name].step(k)

    pa_w, pb_w = (row_weights([x for x in order if x != "zh"], 2) for order in (PA_ORDER, PB_ORDER))
    fa_w, fb_w = (row_weights([x for x in order if x != "y"]) for order in (FA_ORDER, FB_ORDER))
    wo_w, q_w = row_weights(WO_ORDER), row_weights(Q_ORDER)

    for n in range(2):
        h = (1 - t2) if n == 0 else t2
        for w in range(2):
            grad = nn(a.dout_t[HALF * w : HALF * w + HALF, :], a.hid[:, part(h, D)]).astype(BF)
            for i in range(2):
                for e in range(2):
                    piece = grad[2 * OWN * e : 2 * OWN * e + 2 * OWN, HALF * i : HALF * i + HALF]
                    at_a = OWN * (pa_w["x"] * i + pa_w["y"] * w + e)
                    at_b = OWN * (pb_w["x"] * i + pb_w["y"] * w + e)
                    a.gpj[at_a : at_a + OWN, pl.ds(pl.multiple_of(D * h, HALF), HALF)] = piece[:OWN]
                    a.gpj[at_b : at_b + OWN, pl.ds(pl.multiple_of(D * h + HALF, HALF), HALF)] = piece[OWN:]
        if n == 0:
            pb.start(0)
    pa.start(0)

    grad_hidden((far, far_p), True)

    def out_of(g):
        return nn(stack_rows(a.hid, spans_of(blocks_of(g))), a.wproj[...])

    def back_of(g):
        return nt(stack_rows(a.gpre, spans_of(blocks_of(g))), a.wfc[...])

    @pl.when(d >= 0)
    def _():
        out, grad = out_of(0), back_of(0)
        for k in range(2):
            a.obuf[k] = out[SPAN * k : SPAN * k + SPAN].astype(BF)
            o_copy(k).start()
        for k in range(2):
            a.gbuf[k] = grad[SPAN * k : SPAN * k + SPAN].astype(BF)
            g_copy(k).start()

    def weights_fc(n):
        h = lax.rem(n, 2)
        w = lax.div(n, 2)
        ones = jnp.ones((16, SEQ), BF)
        grad = nn(jnp.concatenate([a.wqkv[part(h, HALF), :SEQ], ones], axis=0), a.gpre[:, part(w, D)])
        a.acc_bfc[:, part(w, D)] = grad[HALF : HALF + 1]
        grad = grad.astype(BF)
        for j in range(2):
            for i in range(2):
                piece = grad[OWN * (2 * j + i) : OWN * (2 * j + i) + OWN]
                at_a = fa_w["x"] * i + fa_w["zl"] * j + fa_w["zh"] * h
                at_b = fb_w["x"] * i + fb_w["zl"] * j + fb_w["zh"] * h
                a.dout_t[part(at_a, OWN), part(w, HALF)] = piece[:, :HALF]
                a.gfb[part(at_b, OWN), part(w, HALF)] = piece[:, HALF:]

    loop(4, weights_fc)
    fa.start(0)
    fb.start(0)
    for load in loads_qkv:
        load.start()
    steps(("back", 0))

    @pl.when(d >= 0)
    def _():
        grad_in = back_of(1)
        for k in (1, 0):
            t = blocks_of(1)[k]
            normed, inverse = stats(a.gres[k])
            g_copy(k).wait_recv()
            grad = grad_in[SPAN * k : SPAN * k + SPAN] + a.gin[k].astype(F32)
            wide = a.drow[t].astype(F32)
            branch = (wide + norm_back(grad * a.gain_two[...], normed, inverse)).astype(BF)
            a.gbr[t] = branch
            b_copy(k).start()
            a.acc[0] += jnp.sum(branch.astype(F32), axis=0, keepdims=True)
            a.acc[1] += jnp.sum(wide, axis=0, keepdims=True)
            a.acc[4] += jnp.sum(grad * normed, axis=0, keepdims=True)
            a.acc[5] += jnp.sum(grad, axis=0, keepdims=True)

    steps(("back", 1))

    @pl.when(d >= 0)
    def _():
        out = out_of(1)
        for k in (1, 0):
            o_copy(k).wait_recv()
            g_copy(k).wait_send()
            whole = a.gres[k] + (out[SPAN * k : SPAN * k + SPAN] + a.oin[k].astype(F32)) + a.b_proj[...]
            a.gbuf[k] = whole.astype(BF)
            if k == 1:
                y_far.start()
            else:
                y_own.start()


    spread["ve"].start(early_tiles)

    b_copy(0).wait_recv()
    b_copy(1).wait_recv()

    def branch_block(t):
        rows = pl.ds(mul(t, SPAN), SPAN)
        grad = nt(a.wout[pl.ds(half_c, HALF), :], a.gbr[t])
        for p in range(3):
            parts = []
            for e in range(2):
                head = 2 * p + e
                at = slice(HEAD * head, HEAD * head + HEAD)
                inverse = a.linv[head, :, rows]
                piece = grad[at].astype(BF).astype(F32)
                a.delta[head, :, rows] = inverse * jnp.sum(
                    piece * a.o_t[at, rows].astype(F32), axis=0, keepdims=True
                )
                parts.append(piece * inverse)
            scaled = jnp.concatenate(parts, axis=0).astype(BF)
            a.hid[rows, 3 * HALF + 128 * p : 3 * HALF + 128 * p + 128] = scaled.T

    @pl.when(d >= 0)
    def _():
        for t in range(BLOCKS):
            branch_block(t)

    steps("branch")
    for n in range(2):
        lhs = a.o_t[2 * OWN * n : 2 * OWN * n + 2 * OWN, :]
        grad = nn(lhs[:, :SPAN], a.gbr[0])
        for t in range(1, BLOCKS):
            grad += nn(lhs[:, SPAN * t : SPAN * t + SPAN], a.gbr[t])
        grad = grad.astype(BF)
        for i in range(2):
            for w in range(2):
                at = OWN * (wo_w["zl"] * n + wo_w["x"] * i + wo_w["y"] * w)
                a.wout[at : at + OWN, :HALF] = grad[OWN * i : OWN * i + OWN, HALF * w : HALF * w + HALF]
    wo.start(0)

    def between(p, i):
        for value in range(3):
            if plan["pair", value, i]:

                @pl.when(p == value)
                def _():
                    steps(("pair", value, i))

    def backward_pair(p):
        cols = pl.ds(mul(p, 128), 128)
        do_cols = pl.ds(pl.multiple_of(3 * HALF + 128 * p, 128), 128)
        a.k_t[...] = a.kn[:, cols].T
        masks = [lane < HEAD, lane >= HEAD]

        def rows_of(i):
            return slice(SPAN * i, SPAN * i + SPAN)

        def tile(e, i, j):
            n = i * (i + 1) // 2 + j
            if e == 0:
                return a.wproj.at[pl.ds(SPAN * (n % 6), SPAN), pl.ds(SPAN * (n // 6), SPAN)]
            return a.wfc.at[pl.ds(SPAN * (n % 3), SPAN), pl.ds(SPAN * (n // 3), SPAN)]

        def of_head(ref, i, e, at):
            both = ref[rows_of(i), at]
            return jnp.where(masks[e], both, jnp.zeros_like(both))

        @pl.when(p >= 0)
        def _():
            for i, e in itertools.product(reversed(range(BLOCKS)), range(2)):
                head = 2 * p + e
                delta = a.delta[head, :, rows_of(i)]
                product = nt(a.vn[: SPAN * (i + 1), cols], of_head(a.hid, i, e, do_cols))
                for j in range(i + 1):
                    at = base(i) + SPAN * j
                    weights = a.probs[head, at : at + SPAN, :].astype(F32)
                    tile(e, i, j)[...] = (weights * (product[rows_of(j)] - delta)).astype(BF)

        between(p, 3)

        @pl.when(p >= 0)
        def _():
            for i in reversed(range(BLOCKS)):
                parts = []
                for e in range(2):
                    scores = jnp.concatenate([tile(e, i, j)[...] for j in range(i + 1)], axis=0)
                    parts.append(nn(a.k_t[HEAD * e : HEAD * e + HEAD, : SPAN * (i + 1)], scores))
                a.hid[rows_of(i), cols] = (jnp.concatenate(parts, axis=0) * 0.125).T.astype(BF)

        between(p, 2)

        @pl.when(p >= 0)
        def _():
            for i in reversed(range(BLOCKS)):
                keys = slice(0, SPAN * (i + 1))
                at = base(i)
                scores = [
                    jnp.concatenate([tile(e, i, j)[...] for j in range(i + 1)], axis=0) for e in range(2)
                ]
                weights = [a.probs[2 * p + e, at : at + SPAN * (i + 1), :] for e in range(2)]
                queries = [of_head(a.qn, i, e, cols) for e in range(2)]
                grads = [of_head(a.hid, i, e, do_cols) for e in range(2)]
                part_k = nn(jnp.concatenate(scores, axis=1), jnp.concatenate(queries, axis=0))
                part_v = nn(jnp.concatenate(weights, axis=1), jnp.concatenate(grads, axis=0))
                if i == BLOCKS - 1:
                    a.dk[...] = part_k
                    a.dv[...] = part_v
                else:
                    a.dk[keys, :] += part_k
                    a.dv[keys, :] += part_v

        between(p, 1)
        at_k = pl.ds(pl.multiple_of(HALF + 128 * p, 128), 128)
        at_v = pl.ds(pl.multiple_of(2 * HALF + 128 * p, 128), 128)
        low_k, low_v = a.dk[...].astype(BF), a.dv[...].astype(BF)
        a.hid[:, at_k] = low_k
        a.hid[:, at_v] = low_v

        @pl.when(p >= 0)
        def _():
            both = jnp.concatenate([a.hid[:, cols], a.hid[:, at_k], a.hid[:, at_v]], axis=1)
            ones = jnp.ones((16, SEQ), BF)
            grad = nn(jnp.concatenate([a.ain_t[...], ones], axis=0), both)
            a.acc_qv[0, :, cols] = grad[D : D + 1, :128]
            a.acc_qv[1, :, cols] = grad[D : D + 1, SPAN:]
            grad = grad.astype(BF)
            for h in range(2):
                for j in range(2):
                    for i in range(2):
                        at = (4 * h + 2 * j + i) * OWN
                        to = q_w["zh"] * h + q_w["zl"] * j + q_w["x"] * i
                        a.gpre[OWN * to : OWN * to + OWN, part(p, HALF)] = grad[at : at + OWN]

        for n, (pair, _, _) in enumerate(Q_CHAINS):

            @pl.when(p == pair)
            def _():
                qs[n][0].start(0)

        between(p, -1)

    for p in range(3):
        mix_copy(p).wait_send()
    loop(3, backward_pair)

    a_first = numbers(2)
    for load in loads_qkv:
        load.wait()

    def a_copy(s):
        return remote(a.obuf.at[s], a.oin.at[s], a_first + s, to_core)

    x_far = remote(a.gbuf.at[1], a.gx_out.at[y], numbers(1), to_y)
    x_own = pltpu.make_async_copy(a.gbuf.at[0], a.gx_out.at[y], a.local.at[11])

    def input_pair(g):
        ts = blocks_of(g)
        spans = spans_of(ts)
        part_in = nt(stack_rows(a.hid, spans, slice(0, 3 * HALF)), a.wqkv[...])
        for k in (1, 0):
            half = slice(SPAN * k, SPAN * k + SPAN)
            if g == 0:
                a.obuf[k] = part_in[half].astype(BF)
                a_copy(k).start()
                continue
            normed, inverse = stats(a.xrow[ts[k]].astype(F32))
            a_copy(k).wait_recv()
            grad = part_in[half] + a.oin[k].astype(F32)
            total = a.gbr[ts[k]].astype(F32) + norm_back(grad * a.gain_one[...], normed, inverse)
            a.gbuf[k] = total.astype(BF)
            if k == 1:
                x_far.start()
            else:
                x_own.start()
            a.acc[2] += jnp.sum(grad * normed, axis=0, keepdims=True)
            a.acc[3] += jnp.sum(grad, axis=0, keepdims=True)

    y_far.wait()
    y_own.wait()
    for k in range(2):
        o_copy(k).wait_send()

    for g in range(2):
        input_pair(g)
        steps(("input", g))

    spread["vl"].start(late_tiles)
    steps("last")

    for n, device in enumerate(extra):
        outs = (
            (a.gpj_out, a.xs_pj, a.xr_pj),
            (a.gfc_out, a.xs_fc, a.xr_fc),
            (a.gwo_out, a.xs_wo, a.xr_wo),
        )
        copies = []
        for m, (out, sent, came) in enumerate(outs):
            sent[0] = out[...].astype(BF)
            copies.append((out, sent, came, m))
        a.xs_q[0] = a.gq_out[c].astype(BF)
        copies.append((a.gq_out.at[c], a.xs_q, a.xr_q, 3))
        started = []
        for out, sent, came, m in copies:
            copy = pltpu.make_async_remote_copy(
                src_ref=sent.at[0],
                dst_ref=came.at[n],
                send_sem=a.xsend.at[n, m],
                recv_sem=a.xrecv.at[n, m],
                device_id=device,
                device_id_type=MESH,
            )
            copy.start()
            started.append(copy)
        for (out, sent, came, m), copy in zip(copies, started):
            copy.wait()
            out[...] = (sent[0].astype(F32) + came[n].astype(F32)).astype(out.dtype)
    if extra:
        a.xs_q[0] = a.gq_out[c]
        copy = remote(a.xs_q.at[0], a.xc_q, numbers(1), to_core)
        copy.start()
        copy.wait()
        a.gq_out[other] = a.xc_q[...]

    for copy in pending:
        copy.wait_send()
    for name in ("q1", "q2"):
        chains[name].sent()
    for s in range(2):
        a_copy(s).wait_send()
    b_copy(0).wait_send()
    b_copy(1).wait_send()
    for copy in (x_far, x_own):
        copy.wait()
    assert count[0] <= 120


def finish_kernel(dp, *refs):
    y_in, gx, gq, gwo, gfc, gpj, early, late = refs[:8]
    (y_out, gx_out, gq_out, bq_out, bv_out, gwo_out, bo_out, gfc_out, bf_out, gpj_out) = refs[8:18]
    rest = refs[18:]
    d = lax.axis_index("dp")
    b = lax.axis_index("blk")
    y, c = lax.div(b, 2), lax.rem(b, 2)
    subs = dp // 8
    sub = lax.rem(d, subs)
    rows = D // dp

    def rows_of(v):
        out = v[:rows]
        for n in range(1, subs):
            out = jnp.where(sub == n, v[rows * n : rows * n + rows], out)
        return out

    y_out[...] = y_in[...]
    gx_out[...] = gx[...].astype(F32)

    @pl.when(pl.program_id(0) == 0)
    def _():
        query = [jnp.concatenate([gq[n, p, :, :128] for p in range(3)], axis=1) for n in range(2)]
        key = [jnp.concatenate([gq[n, p, :, 128:256] for p in range(3)], axis=1) for n in range(2)]
        value = [jnp.concatenate([gq[n, p, :, 256:] for p in range(3)], axis=1) for n in range(2)]
        first = jnp.concatenate([query[0], query[1], key[0]], axis=1)
        second = jnp.concatenate([key[1], value[0], value[1]], axis=1)
        full = jnp.where(y == 0, first, second)
        columns = 3 * D // BLOCKS
        full = full.astype(F32)
        gq_out[...] = rows_of(jnp.where(c == 0, full[:, :columns], full[:, columns:]))
        columns = D // BLOCKS
        gwo_out[...] = rows_of(jnp.where(c == 0, gwo[:, :columns], gwo[:, columns:]))
        gfc_out[...] = rows_of(gfc[...])
        cols_ff = 2 * FF // dp
        out = gpj[:, :cols_ff]
        for n in range(1, subs):
            out = jnp.where(sub == n, gpj[:, cols_ff * n : cols_ff * n + cols_ff], out)
        gpj_out[...] = out

        bq_out[...] = late[2, :rows]
        bv_out[...] = late[3, :rows]
        bo_out[...] = early[0, :rows]
        units = 2 * FF // dp
        pieces = [early[4 + n : 5 + n, : min(128, units - 128 * n)] for n in range(-(-units // 128))]
        bf_out[...] = jnp.concatenate(pieces, axis=1)[0]
        for out, v in zip(rest, (early[1], late[0], late[1], early[2], early[3])):
            out[...] = v[:rows]


def body(dp, layer_input, lengths, w_qkv, b_query, b_value, w_out, b_out, w_fc, b_fc, w_proj, b_proj, *more):
    d_out = more[4]
    vectors = (b_query, b_value, b_out, b_proj) + more[:4] + (b_fc,)
    args = (layer_input, lengths, w_qkv, w_out, w_fc, w_proj, d_out) + vectors
    shapes = scratch(dp)
    spaces = [pl.ANY, pltpu.SMEM] + [pl.ANY] * 5 + [pltpu.VMEM] * len(VECTORS)
    in_specs = [pl.BlockSpec(memory_space=space) for space in spaces]
    out_shape = (
        jax.ShapeDtypeStruct((2, SPAN, D), BF),
        jax.ShapeDtypeStruct((2, SPAN, D), BF),
        jax.ShapeDtypeStruct((2, 3, OWN, HALF), BF),
        jax.ShapeDtypeStruct((OWN, HALF), F32),
        jax.ShapeDtypeStruct((OWN, D), F32),
        jax.ShapeDtypeStruct((HALF // 2, HALF), F32),
        jax.ShapeDtypeStruct((8, 128), F32),
        jax.ShapeDtypeStruct((8, 128), F32),
    )
    out_specs = [pl.BlockSpec(memory_space=pl.ANY)] * 2 + [pl.BlockSpec(memory_space=pltpu.VMEM)] * 6
    outs = pl.pallas_call(
        functools.partial(kernel, dp, INPUTS + OUTPUTS + tuple(shapes)),
        out_shape=out_shape,
        in_specs=in_specs,
        out_specs=out_specs,
        scratch_shapes=list(shapes.values()),
        compiler_params=pltpu.CompilerParams(
            collective_id=0, has_side_effects=True, vmem_limit_bytes=63 * 1024 * 1024
        ),
    )(*args)
    rows = D // dp
    line = jax.ShapeDtypeStruct((rows,), F32)
    out_shape = (
        jax.ShapeDtypeStruct((2, SPAN, D), BF),
        jax.ShapeDtypeStruct((2, SPAN, D), F32),
        jax.ShapeDtypeStruct((rows, 3 * D // BLOCKS), F32),
        line,
        line,
        jax.ShapeDtypeStruct((rows, D // BLOCKS), F32),
        line,
        jax.ShapeDtypeStruct((rows, D), F32),
        jax.ShapeDtypeStruct((2 * FF // dp,), F32),
        jax.ShapeDtypeStruct((D // BLOCKS, 2 * FF // dp), F32),
    ) + (line,) * 5

    def specs(arrays):
        by_row = pl.BlockSpec((1, SPAN, D), lambda n: (n, 0, 0))
        return [by_row, by_row] + [
            pl.BlockSpec(v.shape, lambda n, rank=len(v.shape): (0,) * rank) for v in arrays[2:]
        ]

    done = pl.pallas_call(
        functools.partial(finish_kernel, dp),
        grid=(2,),
        out_shape=out_shape,
        in_specs=specs(outs),
        out_specs=specs(out_shape),
        compiler_params=pltpu.CompilerParams(vmem_limit_bytes=63 * 1024 * 1024),
    )(*outs)
    return tuple(done[:9]) + (done[9].T,) + tuple(done[10:])


def solution(mesh):
    rows = P("dp", "blk", None)
    grid = P("dp", "blk")
    line = P("dp")
    in_specs = (rows, P("dp", None)) + (P(),) * 13 + (rows,)
    out_specs = (rows, rows, grid, line, line, grid, line, grid, line, grid) + (line,) * 5
    dp = mesh.shape["dp"]
    return jax.shard_map(
        functools.partial(body, dp),
        mesh=mesh,
        in_specs=in_specs,
        out_specs=out_specs,
        check_vma=False,
    )
```

```python
import functools
import itertools

import jax
import jax.numpy as jnp
from jax import lax
from jax.experimental import pallas as pl
from jax.experimental.pallas import tpu as pltpu
from jax.sharding import PartitionSpec as P

HEADS = 12
HEAD = 64

ln_epsilon = 1e-05
gelu_factor = 0.7978845608028654
big_negative = -1e30

BF = jnp.bfloat16
F32 = jnp.float32
MESH = pl.DeviceIdType.MESH

SPAN = 256
BLOCKS = 4
SEQ = SPAN * BLOCKS
D = 768
HALF = D // 2
FF = 1536
CHUNK = 512
OWN = 96

PA_ORDER = ("x", "zh", "y")
PB_ORDER = ("zh", "y", "x")
FA_ORDER = ("zl", "y", "x", "zh")
FB_ORDER = ("y", "zl", "x", "zh")
WO_ORDER = ("y", "zl", "x")
Q_ORDER = ("x", "zl", "zh")
Q_CHAINS = ((0, 0, 3), (1, 0, 3), (2, 0, 3))


PLACES = (
    [("back", n) for n in range(2)]
    + ["branch"]
    + [("pair", p, i) for p in range(3) for i in (3, 2, 1, 0, -1)]
    + [("input", n) for n in range(2)]
    + ["last"]
)
STEPS = {
    "branch": ["pa"],
    ("pair", 0, -1): ["ve"],
    ("pair", 1, 3): ["ve"],
    ("pair", 1, -1): ["pb", "fa", "fb", "q0"],
    ("pair", 2, 3): ["pa"],
    ("pair", 2, -1): ["wo", "q1", "q0"],
    ("input", 1): ["fb"],
    "last": (
        ["q2", "q0", "pa", "pa", "vl", "fb", "wo", "pb", "q1", "fa", "vl", "q0", "q0", "wo", "q2", "pa", "wo"]
        + ["pb", "fa", "fb", "pb", "q1", "pb", "wo", "fa", "sent", "q2", "q1", "q1"]
    ),
}


def numbered():
    seen, out = {}, {}
    for place in PLACES:
        names = list(STEPS.get(place, ()))
        out[place] = []
        for name in names:
            out[place].append((name, seen.get(name, 0)))
            seen[name] = seen.get(name, 0) + 1
    return out


def proj_lands(order):
    rows, halves, shapes = D, 2, []
    for axis in order:
        if axis == "zh":
            halves = 1
        else:
            rows //= 2
        shapes.append((halves, rows, HALF))
    return shapes + [(2, OWN, HALF), (OWN, HALF)]


def fc_lands(order):
    rows, cols, shapes = D, D, []
    for axis in order:
        if axis == "y":
            cols //= 2
        else:
            rows //= 2
        shapes.append((rows, cols))
    return shapes


def row_lands(order, cols):
    return [(D >> (n + 1), cols) for n in range(len(order))]


def row_weights(order, last=1):
    return {axis: last << (len(order) - 1 - n) for n, axis in enumerate(order)}


def stats(v):
    centre = jnp.mean(v, axis=-1, keepdims=True)
    centered = v - centre
    inverse = lax.rsqrt(jnp.mean(centered * centered, axis=-1, keepdims=True) + ln_epsilon)
    return centered * inverse, inverse


def norm_back(grad_norm, normed, inverse):
    first = jnp.mean(grad_norm, axis=-1, keepdims=True)
    second = jnp.mean(grad_norm * normed, axis=-1, keepdims=True)
    return inverse * (grad_norm - first - normed * second)


def nn(a, b):
    return jnp.dot(a, b, preferred_element_type=F32)


def nt(a, b):
    return lax.dot_general(a, b, (((1,), (1,)), ((), ())), preferred_element_type=F32)


def mul(i, n):
    return pl.multiple_of(i * n, n)


def loop(n, body):
    def step(i, carry):
        body(i)
        return carry

    lax.fori_loop(0, n, step, 0)


def gelu_both(v):
    square = v * v
    inner = jnp.tanh(v * (gelu_factor + 0.044715 * gelu_factor * square))
    half = 0.5 + 0.5 * inner
    value = v * half
    return value, half + value * ((1.0 - inner) * (gelu_factor + 3.0 * 0.044715 * gelu_factor * square))


def top_of(v):
    while v.shape[0] > 8:
        half = v.shape[0] // 2
        v = jnp.maximum(v[:half], v[half:])
    return v


def ahead(items, product):
    items = list(items)
    coming = product(*items[0])
    for n, item in enumerate(items):
        here = coming
        if n + 1 < len(items):
            coming = product(*items[n + 1])
        yield item, here


def base(i):
    return SPAN * (i * (i + 1) // 2)


def scratch(dp):
    extras = max(0, dp.bit_length() - 4)
    vm = pltpu.VMEM
    shapes = dict(
        xrow=vm((BLOCKS, SPAN, D), BF),
        drow=vm((BLOCKS, SPAN, D), BF),
        wqkv=vm((D, 3 * HALF), BF),
        wout=vm((D, D), BF),
        wfc=vm((D, FF), BF),
        wproj=vm((FF, D), BF),
        bfc=vm((1, FF), F32),
        ain_t=vm((D, SEQ), BF),
        qn=vm((SEQ, HALF), BF),
        kn=vm((SEQ, HALF), BF),
        vn=vm((SEQ, HALF), BF),
        k_t=vm((128, SEQ), BF),
        v_t=vm((6, HEAD + 16, SEQ), BF),
        start=vm((BLOCKS, 1, SPAN), jnp.int32),
        probs=vm((6, base(4), SPAN), BF),
        linv=vm((6, 1, SEQ), F32),
        delta=vm((6, 1, SEQ), F32),
        o_t=vm((HALF, SEQ), BF),
        mix=vm((2, SEQ, HALF), BF),
        gpj=vm((D, FF), BF),
        gfb=vm((D, D), BF),
        vectors=vm((1, 8 * D + 2 * FF), F32),
        dout_t=vm((D, SEQ), BF),
        hid=vm((SEQ, FF), BF),
        gpre=vm((SEQ, FF), BF),
        obuf=vm((2, SPAN, D), BF),
        oin=vm((2, SPAN, D), BF),
        gbuf=vm((2, SPAN, D), BF),
        gin=vm((2, SPAN, D), BF),
        gres=vm((2, SPAN, D), F32),
        gbr=vm((BLOCKS, SPAN, D), BF),
        dk=vm((SEQ, 128), F32),
        dv=vm((SEQ, 128), F32),
        acc_bfc=vm((1, FF), F32),
        acc_qv=vm((2, 1, HALF), F32),
        acc=vm((6, 1, D), F32),
    )
    for name in ("early", "late"):
        shapes.update(
            {
                name: vm((dp, 8, 128), F32),
                name + "_r": vm((dp, 8, 128), F32),
                name + "_s": vm((8, 128), F32),
                name + "_q": vm((3, 8, 128), F32),
                name + "_send": pltpu.SemaphoreType.DMA((dp + 3,)),
                name + "_recv": pltpu.SemaphoreType.DMA((dp + 3,)),
            }
        )
    shapes.update(
        local=pltpu.SemaphoreType.DMA((16,)),
        send=pltpu.SemaphoreType.DMA((120,)),
        recv=pltpu.SemaphoreType.DMA((120,)),
    )
    lands = dict(
        pa=proj_lands(PA_ORDER),
        pb=proj_lands(PB_ORDER),
        fa=fc_lands(FA_ORDER),
        fb=fc_lands(FB_ORDER),
        wo=row_lands(WO_ORDER, HALF) + [(2, OWN, HALF), (OWN, HALF)],
    )
    for n, (_, _, units) in enumerate(Q_CHAINS):
        cols = 128 * units
        if n < 2:
            lands[f"q{n}"] = row_lands(Q_ORDER, cols) + [(OWN, cols)] * 3
        else:
            lands[f"q{n}"] = [(4 * OWN, cols), (3, OWN, cols), (3, OWN, cols)]
    for name, sizes in lands.items():
        for n, size in enumerate(sizes):
            shapes[f"{name}_{n}"] = vm(size, BF)
    if extras:
        shapes.update(
            xs_pj=vm((1, HALF // 2, HALF), BF),
            xr_pj=vm((extras, HALF // 2, HALF), BF),
            xs_fc=vm((1, OWN, D), BF),
            xr_fc=vm((extras, OWN, D), BF),
            xs_wo=vm((1, OWN, HALF), BF),
            xr_wo=vm((extras, OWN, HALF), BF),
            xs_q=vm((1, 3, OWN, HALF), BF),
            xr_q=vm((extras, 3, OWN, HALF), BF),
            xc_q=vm((3, OWN, HALF), BF),
            xsend=pltpu.SemaphoreType.DMA((extras, 4)),
            xrecv=pltpu.SemaphoreType.DMA((extras, 4)),
        )
    return shapes


VECTORS = ("b_query", "b_value", "b_out", "b_proj", "gain_one", "shift_one", "gain_two", "shift_two", "b_fc")
INPUTS = ("x_in", "lengths", "w_qkv", "w_out", "w_fc", "w_proj", "d_in") + tuple(n + "_in" for n in VECTORS)
OUTPUTS = ("y_out", "gx_out", "gq_out", "gwo_out", "gfc_out", "gpj_out", "early_out", "late_out")


def kernel(dp, names, *refs):
    r = dict(zip(names, refs))
    a = type("Refs", (), r)
    for n, name in enumerate(VECTORS):
        size = 2 * FF if name == "b_fc" else D
        a.vectors[:, D * n : D * n + size] = r[name + "_in"][...].reshape(1, size)
        setattr(a, name, a.vectors.at[:, D * n : D * n + size])
    d = lax.axis_index("dp")
    b = lax.axis_index("blk")
    y = lax.div(b, 2)
    c = lax.rem(b, 2)
    other = 1 - c

    def bit(weight):
        return lax.rem(lax.div(d, weight), 2)

    def across(weight):
        return (d + weight * (1 - 2 * bit(weight)), b)

    t2, t1, t0 = bit(dp // 2), bit(dp // 4), bit(dp // 8)
    to_core = (d, 2 * y + other)
    to_y = (d, 2 * (1 - y) + c)
    to2, to1, to0 = across(dp // 2), across(dp // 4), across(dp // 8)
    to21 = (to2[0] + to1[0] - d, b)
    to_diagonal = (d, 2 * (1 - y) + other)
    groups = [(lax.rem(d + n, dp), b) for n in range(1, dp)]
    extra = []
    weight = dp // 16
    while weight >= 1:
        extra.append(across(weight))
        weight //= 2

    count = [0]

    def numbers(n):
        count[0] += n
        return count[0] - n

    def remote(src, dst, number, device):
        return pltpu.make_async_remote_copy(
            src_ref=src,
            dst_ref=dst,
            send_sem=a.send.at[number],
            recv_sem=a.recv.at[number],
            device_id=device,
            device_id_type=MESH,
        )

    pending = []

    def post(src, dst, device):
        copy = remote(src, dst, numbers(1), device)
        copy.start()
        pending.append(copy)
        return copy

    barrier = pltpu.get_barrier_semaphore()
    partners = [to_core, to_y, to_diagonal] + groups
    for device in partners:
        pl.semaphore_signal(barrier, inc=1, device_id=device, device_id_type=MESH)
    pl.semaphore_wait(barrier, len(partners))

    far = 2 * (1 - y) + c
    near_p = 2 * y + other
    far_p = 2 * (1 - y) + other
    x_y = post(a.x_in.at[1 - y], a.xrow.at[b], to_y)
    x_c = post(a.x_in.at[y], a.xrow.at[b], to_core)
    x_l = pltpu.make_async_copy(a.x_in.at[y], a.xrow.at[b], a.local.at[0])
    x_l.start()
    half_c = mul(c, HALF)
    loads_qkv = []
    for u in range(3):
        loads_qkv.append(
            pltpu.make_async_copy(
                a.w_qkv.at[:, pl.ds(pl.multiple_of(D * u + c * HALF, 128), HALF)],
                a.wqkv.at[:, pl.ds(HALF * u, HALF)],
                a.local.at[1 + u],
            )
        )
    loads_mlp = [pltpu.make_async_copy(a.w_out, a.wout, a.local.at[4])]
    for h in range(2):
        ff_at = pl.ds(pl.multiple_of(h * FF + c * D, 128), D)
        loads_mlp.append(
            pltpu.make_async_copy(a.w_fc.at[:, ff_at], a.wfc.at[:, pl.ds(h * D, D)], a.local.at[5 + h])
        )
        loads_mlp.append(
            pltpu.make_async_copy(a.w_proj.at[ff_at], a.wproj.at[pl.ds(h * D, D)], a.local.at[7 + h])
        )
        a.bfc[:, h * D : h * D + D] = a.b_fc[:, ff_at]
    d_l = pltpu.make_async_copy(a.d_in.at[y], a.drow.at[b], a.local.at[9])
    for load in loads_qkv + [d_l] + loads_mlp:
        load.start()
    d_y = remote(a.d_in.at[1 - y], a.drow.at[b], numbers(1), to_y)
    pending.append(d_y)
    d_c = post(a.d_in.at[y], a.drow.at[b], to_core)

    position = lax.broadcasted_iota(jnp.int32, (1, SPAN), 1)
    for i in range(BLOCKS):
        begin = jnp.zeros((1, SPAN), jnp.int32)
        total = jnp.int32(0)
        for j in range(8):
            total = total + a.lengths[y, j]
            begin = jnp.where(position + SPAN * i >= total, total, begin)
        a.start[i] = begin
    a.acc[...] = jnp.zeros_like(a.acc)
    a.v_t[:, HEAD:, :] = jnp.ones((6, 16, SEQ), BF)

    for load in loads_qkv:
        load.wait()
    bias_q = a.b_query[:, pl.ds(half_c, HALF)]
    bias_v = a.b_value[:, pl.ds(half_c, HALF)]

    def project(t):
        rows = pl.ds(mul(t, SPAN), SPAN)
        normed, _ = stats(a.xrow[t].astype(F32))
        low = (normed * a.gain_one[...] + a.shift_one[...]).astype(BF)
        out = nn(low, a.wqkv[...])
        a.qn[rows, :] = ((out[:, :HALF] + bias_q).astype(BF).astype(F32) * 0.125).astype(BF)
        values = (out[:, 2 * HALF :] + bias_v).astype(BF)
        turned = values.T
        a.kn[rows, :] = out[:, HALF : 2 * HALF].astype(BF)
        a.vn[rows, :] = values
        for h in range(6):
            a.v_t[h, :HEAD, rows] = turned[HEAD * h : HEAD * h + HEAD]

    def turn(t):
        rows = pl.ds(mul(t, SPAN), SPAN)
        normed, _ = stats(a.xrow[t].astype(F32))
        a.ain_t[:, rows] = (normed * a.gain_one[...] + a.shift_one[...]).astype(BF).T

    def turn_d(t):
        a.dout_t[:, pl.ds(mul(t, SPAN), SPAN)] = a.drow[t].T

    def stack(ref, ts):
        return jnp.concatenate([ref[t] for t in ts], axis=0)

    def stack_rows(ref, spans, cols=slice(None)):
        return jnp.concatenate([ref[rows, cols] for rows in spans], axis=0)

    def spans_of(ts):
        return [pl.ds(mul(t, SPAN), SPAN) for t in ts]

    def grad_hidden(ts, slopes):
        spans = spans_of(ts)
        top = stack(a.drow, ts)
        for f in range(0, FF, CHUNK):
            here = slice(f, f + CHUNK)
            grad = nt(top, a.wproj[here, :])
            if slopes:
                grad = grad * stack_rows(a.gpre, spans, here).astype(F32)
            grad = grad.astype(BF)
            for k, rows in enumerate(spans):
                a.gpre[rows, here] = grad[SPAN * k : SPAN * k + SPAN]

    fwd_x = remote(a.xrow.at[far], a.xrow.at[far], numbers(1), to_core)
    fwd_d = remote(a.drow.at[far], a.drow.at[far], numbers(1), to_core)
    pending += [fwd_x, fwd_d]

    def arrive(s):
        @pl.when(s == 0)
        def _():
            x_l.wait()

        @pl.when(s == 1)
        def _():
            x_c.wait_recv()

        @pl.when(s == 2)
        def _():
            x_y.wait_recv()
            fwd_x.start()
            d_y.start()

        @pl.when(s == 3)
        def _():
            fwd_x.wait_recv()

        far_s = lax.div(s, 2)
        core_s = lax.rem(s, 2)
        t = 2 * (y + far_s * (1 - 2 * y)) + c + core_s * (1 - 2 * c)
        project(t)

        @pl.when(s == 0)
        def _():
            d_l.wait()

        @pl.when(s == 1)
        def _():
            d_c.wait_recv()

            for load in loads_mlp:
                load.wait()

        @pl.when(s < 2)
        def _():
            turn(t)
            turn_d(t)

        @pl.when(s == 1)
        def _():
            grad_hidden((b, near_p), False)

    loop(4, arrive)

    lane = lax.broadcasted_iota(jnp.int32, (1, 128), 1)
    key_index = lax.broadcasted_iota(jnp.int32, (SPAN, SPAN), 0)
    query_index = lax.broadcasted_iota(jnp.int32, (SPAN, SPAN), 1)
    mix_first = numbers(3)

    def mix_copy(p):
        here = a.mix.at[c, :, pl.ds(mul(p, 128), 128)]
        return remote(here, here, mix_first + p, to_core)

    def forward_pair(p):
        cols = pl.ds(mul(p, 128), 128)
        masks = [lane < HEAD, lane >= HEAD]

        def score(i, e):
            pair = a.qn[SPAN * i : SPAN * i + SPAN, cols]
            return nt(a.kn[: SPAN * (i + 1), cols], jnp.where(masks[e], pair, jnp.zeros_like(pair)))

        def weigh(i, e):
            head = 2 * p + e
            feats = pl.ds(mul(head, HEAD), HEAD)
            rows = slice(SPAN * i, SPAN * i + SPAN)
            keys_n = SPAN * (i + 1)
            out = nn(a.v_t[head, :, :keys_n], a.probs[head, base(i) : base(i) + keys_n, :])
            inverse = 1.0 / out[HEAD : HEAD + 1]
            a.linv[head, :, rows] = inverse
            a.o_t[feats, rows] = (out[:HEAD] * inverse).astype(BF)

        late = []
        for (i, e), product in ahead(itertools.product(range(BLOCKS), range(2)), score):
            head = 2 * p + e
            begin = a.start[i]
            scores, tops = [], []
            for j in range(i + 1):
                s = product[SPAN * j : SPAN * j + SPAN]
                ok = key_index + SPAN * j >= begin
                if j == i:
                    ok = ok & (key_index <= query_index)
                s = jnp.where(ok, s, big_negative)
                scores.append(s)
                tops.append(top_of(s))
            top = tops[0]
            for here in tops[1:]:
                top = jnp.maximum(top, here)
            top = jnp.max(top, axis=0, keepdims=True)
            for j in range(i + 1):
                at = base(i) + SPAN * j
                a.probs[head, at : at + SPAN, :] = jnp.exp(scores[j] - top).astype(BF)
            late.append((i, e))
            if len(late) > 1:
                weigh(*late.pop(0))

        for item in late:
            weigh(*item)

        a.mix[c, :, cols] = a.o_t[pl.ds(mul(p, 128), 128), :].T
        mix_copy(p).start()

        @pl.when(p == 2)
        def _():
            d_y.wait_recv()
            fwd_d.start()

    loop(3, forward_pair)
    turn(far)
    turn(far_p)

    for p in range(3):
        mix_copy(p).wait_recv()

    o_first, g_first, b_first = numbers(2), numbers(2), numbers(2)

    def o_copy(s):
        return remote(a.obuf.at[s], a.oin.at[s], o_first + s, to_core)

    def g_copy(s):
        return remote(a.gbuf.at[s], a.gin.at[s], g_first + s, to_core)

    def b_copy(k):
        t = far if k else b
        return remote(a.gbr.at[t], a.gbr.at[t], b_first + k, to_core)

    y_far = remote(a.gbuf.at[1], a.y_out.at[y], numbers(1), to_y)
    y_own = pltpu.make_async_copy(a.gbuf.at[0], a.y_out.at[y], a.local.at[10])

    def blocks_of(g):
        core = other + g * (2 * c - 1)
        return 2 * y + core, 2 * (1 - y) + core

    def layer_pair(g):
        ts = blocks_of(g)
        spans = spans_of(ts)
        mixed = jnp.concatenate([stack_rows(a.mix.at[n], spans) for n in range(2)], axis=1)
        residual = stack(a.xrow, ts).astype(F32) + nn(mixed, a.wout[...]) + a.b_out[...]
        normed, _ = stats(residual)
        low = (normed * a.gain_two[...] + a.shift_two[...]).astype(BF)
        for k, rows in enumerate(spans):
            a.wqkv[:, rows] = low[SPAN * k : SPAN * k + SPAN].T
        def hidden(f):
            return nn(low, a.wfc[:, f : f + CHUNK])

        for (f,), product in ahead(((f,) for f in range(0, FF, CHUNK)), hidden):
            here = slice(f, f + CHUNK)
            value, slope = gelu_both(product + a.bfc[:, here])
            value = value.astype(BF)
            a.hid[spans[0], here] = value[:SPAN]
            a.hid[spans[1], here] = value[SPAN:]
            a.gpre[spans[0], here] = (slope[:SPAN] * a.gpre[spans[0], here].astype(F32)).astype(BF)
            a.gpre[spans[1], here] = slope[SPAN:].astype(BF)

        @pl.when(g == 1)
        def _():
            a.gres[0] = residual[:SPAN]
            a.gres[1] = residual[SPAN:]

    loop(2, layer_pair)
    fwd_d.wait_recv()
    turn_d(far)
    turn_d(far_p)

    def part(first, size, n=1):
        return pl.ds(pl.multiple_of(first * size, size), n * size)

    class Chain:
        def __init__(self, stages):
            self.stages = [one_copy(*stage) if len(stage) == 4 else stage for stage in stages]
            self.first = [numbers(len(stage[0])) for stage in self.stages]

        def copies(self, k):
            pieces, _, device = self.stages[k]
            made = [piece() for piece in pieces]
            return [
                remote(piece[0], piece[1], self.first[k] + n, piece[2] if device is None else device)
                for n, piece in enumerate(made)
            ]

        def start(self, k):
            for copy in self.copies(k):
                copy.start()

        def arrive(self, k):
            for copy in self.copies(k):
                copy.wait_recv()

        def step(self, k):
            self.arrive(k)
            keep = self.stages[k][1]
            if keep is not None:
                keep()
            self.start(k + 1)

        def sent(self):
            for k in range(len(self.stages)):
                for copy in self.copies(k):
                    copy.wait_send()

    def plus(keep, came):
        kept, landed = keep(), came()
        kept[...] = kept[...] + landed[...]

    def one_copy(out, land, keep, device):
        landing = land if callable(land) else lambda: land
        return [lambda: (out(), landing())], (lambda: plus(keep, landing)) if keep else None, device

    axes = dict(x=(t0, to0), zl=(t1, to1), zh=(t2, to2), y=(y, to_y))

    def lands_of(name, n):
        return [r[f"{name}_{k}"] for k in range(n)]

    def proj_chain(name, first, order):
        lands = lands_of(name, 5)
        own, last = lands[3], lands[4]

        def at(block, n, h):
            rows = pl.ds(pl.multiple_of(OWN * block, OWN), OWN * n)
            return a.gpj.at[rows, pl.ds(pl.multiple_of(D * h + first, HALF), HALF)]

        stages = []
        start, width, halves = 0, 8, (0, 1)
        for k, axis in enumerate(order):
            mine, device = axes[axis]
            if axis == "zh":
                pairs = [(start, width, 1 - mine, start, mine)]
                halves = (mine,)
            else:
                width //= 2
                gone, kept = start + (1 - mine) * width, start + mine * width
                pairs = [(gone, width, h, kept, h) for h in halves]
                start = kept
            pieces = [
                lambda p=p, k=k, n=n: (at(p[0], p[1], p[2]), lands[k].at[n]) for n, p in enumerate(pairs)
            ]

            def keep(pairs=pairs, k=k, final=k == len(order) - 1, start=start):
                for n, p in enumerate(pairs):
                    plus(lambda: at(p[3], p[1], p[4]), lambda: lands[k].at[n])
                if final:
                    own[c] = at(start + c, 1, t2)[...]

            stages.append((pieces, keep, device))
        stages.append(([lambda: (at(start + other, 1, t2), own.at[c])], None, to_core))
        stages.append(([lambda: (own.at[1 - t1], last)], None, to1))
        return Chain(stages)

    pa = proj_chain("pa", 0, PA_ORDER)
    pb = proj_chain("pb", HALF, PB_ORDER)

    def fc_chain(name, buf, order):
        lands = lands_of(name, 4)

        def at(block, n, w):
            rows = pl.ds(pl.multiple_of(OWN * block, OWN), OWN * n)
            if w is None:
                return buf.at[rows, pl.ds(0, D)]
            return buf.at[rows, part(w, HALF)]

        stages = []
        start, width, side = 0, 8, None
        for k, axis in enumerate(order):
            mine, device = axes[axis]
            if axis == "y":
                gone, kept = (start, width, 1 - y), (start, width, y)
                side = y
            else:
                width //= 2
                gone, kept = (start + (1 - mine) * width, width, side), (start + mine * width, width, side)
                start = kept[0]
            final = k == len(order) - 1
            stages.append(
                (
                    lambda gone=gone: at(*gone),
                    lands[k],
                    None if final else lambda kept=kept: at(*kept),
                    device,
                )
            )
        return Chain(stages), lambda: at(start, 1, y), lands[-1]

    fa, fa_own, fa_last = fc_chain("fa", a.dout_t, FA_ORDER)
    fb, fb_own, fb_last = fc_chain("fb", a.gfb, FB_ORDER)

    def row_stages(at, order, lands):
        stages = []
        start, width = 0, 8
        for k, axis in enumerate(order):
            mine, device = axes[axis]
            width //= 2
            gone, kept = start + (1 - mine) * width, start + mine * width
            stages.append(
                (
                    lambda gone=gone, width=width: at(gone, width),
                    lands[k],
                    lambda kept=kept, width=width: at(kept, width),
                    device,
                )
            )
            start = kept
        return stages, lambda: at(start, 1)

    wo_lands = lands_of("wo", 5)
    wo_stages, wo_own = row_stages(
        lambda block, n: a.wout.at[pl.ds(pl.multiple_of(OWN * block, OWN), OWN * n), pl.ds(0, HALF)],
        WO_ORDER,
        wo_lands,
    )

    def wo_keep():
        kept = wo_own()
        total = (kept[...].astype(F32) + wo_lands[2][...].astype(F32)).astype(BF)
        kept[...] = total
        wo_lands[3][c] = total

    wo = Chain(
        wo_stages[:2]
        + [
            ([lambda: (wo_stages[2][0](), wo_lands[2])], wo_keep, wo_stages[2][3]),
            (wo_own, lambda: wo_lands[3].at[c], None, to_core),
            (lambda: wo_lands[3].at[1 - t2], wo_lands[4], None, to2),
        ]
    )

    def q_chain(n):
        p, first, units = Q_CHAINS[n]
        cols = slice(HALF * p + 128 * first, HALF * p + 128 * (first + units))

        def at(block, n_blocks):
            return a.gpre.at[pl.ds(pl.multiple_of(OWN * block, OWN), OWN * n_blocks), cols]

        def put(core, value):
            a.gq_out[core, p, :, pl.ds(128 * first, 128 * units)] = value

        if n >= 2:
            came_x, came_z, came = lands_of(f"q{n}", 3)
            start = 4 * t0
            own = lambda: at(start + 2 * t1 + t2, 1)
            around = ((2 * (1 - t1) + t2, to1), (2 * t1 + 1 - t2, to2), (2 * (1 - t1) + 1 - t2, to21))

            def keep_z():
                total = own()[...].astype(F32)
                for m in range(3):
                    total = total + came_z[m].astype(F32)
                own()[...] = total.astype(BF)

            def finish():
                chain.arrive(2)
                put(c, own()[...] + came[0])
                put(other, came[1] + came[2])

            chain = Chain(
                [
                    (lambda: at(4 * (1 - t0), 4), came_x, lambda: at(start, 4), to0),
                    (
                        [
                            lambda m=m, block=block, device=device: (at(start + block, 1), came_z.at[m], device)
                            for m, (block, device) in enumerate(around)
                        ],
                        keep_z,
                        None,
                    ),
                    (
                        [
                            lambda m=m, device=device: (own(), came.at[m], device)
                            for m, device in enumerate((to_y, to_core, to_diagonal))
                        ],
                        None,
                        None,
                    ),
                ]
            )
            return chain, finish
        lands = lands_of(f"q{n}", 6)
        stages, own = row_stages(at, Q_ORDER, lands)

        def keep_y():
            lands[5][...] = own()[...] + lands[3][...]

        def finish():
            chain.arrive(4)
            put(c, lands[5][...])
            put(other, lands[4][...])

        chain = Chain(
            stages + [([lambda: (own(), lands[3])], keep_y, to_y), (lambda: lands[5], lands[4], None, to_core)]
        )
        return chain, finish

    class Spread:
        def __init__(self, name, out):
            self.own, self.came, self.sum, self.row, self.send, self.recv = (
                r[name + end] for end in ("", "_r", "_s", "_q", "_send", "_recv")
            )
            self.out = out

        def copy(self, src, dst, number, device):
            return pltpu.make_async_remote_copy(
                src_ref=src,
                dst_ref=dst,
                send_sem=self.send.at[number],
                recv_sem=self.recv.at[number],
                device_id=device,
                device_id_type=MESH,
            )

        def to_groups(self):
            return [self.copy(self.own.at[to[0]], self.came.at[n + 1], n, to) for n, to in enumerate(groups)]

        def to_row(self):
            row = (to_core, to_y, to_diagonal)
            return [self.copy(self.sum, self.row.at[n], dp - 1 + n, to) for n, to in enumerate(row)]

        def start(self, tiles):
            for e in range(dp):
                pieces = [
                    jnp.concatenate([v, jnp.zeros((1, 128 - v.shape[1]), F32)], axis=1) if v.shape[1] < 128 else v
                    for v in tiles(e)
                ]
                pieces += [jnp.zeros((8 - len(pieces), 128), F32)]
                self.own[e] = jnp.concatenate(pieces, axis=0)
            for copy in self.to_groups():
                copy.start()

        def step(self, k):
            if k == 0:
                for copy in self.to_groups():
                    copy.wait_recv()
                total = self.own[d]
                for n in range(1, dp):
                    total = total + self.came[n]
                self.sum[...] = total
                for copy in self.to_row():
                    copy.start()
            else:
                for copy in self.to_row():
                    copy.wait_recv()
                self.out[...] = self.sum[...] + self.row[0] + self.row[1] + self.row[2]

        def sent(self):
            for copy in self.to_groups() + self.to_row():
                copy.wait_send()

    spread = dict(ve=Spread("early", a.early_out), vl=Spread("late", a.late_out))
    share, share_ff = D // dp, 2 * FF // dp

    def early_tiles(e):
        rows = [a.acc[n, :, share * e : share * e + share] for n in (0, 1, 4, 5)]
        at = share_ff * e
        mine = (c == (at % FF) // D).astype(F32)
        at = at // FF * D + at % D
        for n in range(0, share_ff, 128):
            rows.append(a.acc_bfc[:, at + n : at + min(n + 128, share_ff)] * mine)
        return rows

    def late_tiles(e):
        half_dp = dp // 2
        mine = (c == e // half_dp).astype(F32)
        at, at_half = share * e, share * (e % half_dp)
        rows = [a.acc[n, :, at : at + share] for n in (2, 3)]
        return rows + [a.acc_qv[n, :, at_half : at_half + share] * mine for n in range(2)]

    qs = [q_chain(n) for n in range(len(Q_CHAINS))]

    def finish(chain, out, keep, land):
        chain.arrive(len(chain.stages) - 1)
        out[...] = keep[...].astype(F32) + land[...].astype(F32)

    chains = dict(pa=pa, pb=pb, fa=fa, fb=fb, wo=wo)
    last_steps = dict(
        pa=lambda: finish(pa, a.gpj_out.at[pl.ds(0, OWN)], r["pa_3"].at[t1], r["pa_4"]),
        pb=lambda: finish(pb, a.gpj_out.at[pl.ds(OWN, OWN)], r["pb_3"].at[t1], r["pb_4"]),
        fa=lambda: finish(fa, a.gfc_out.at[:, pl.ds(0, HALF)], fa_own(), fa_last),
        fb=lambda: finish(fb, a.gfc_out.at[:, pl.ds(HALF, HALF)], fb_own(), fb_last),
        wo=lambda: finish(wo, a.gwo_out, wo_lands[3].at[t2], wo_lands[4]),
    )
    for n, name in enumerate(("q0", "q1", "q2")):
        chains[name], last_steps[name] = qs[n]
    plan = numbered()
    assert sum(len(todo) for todo in plan.values()) == 5 + sum(len(chain.stages) for chain in chains.values())

    early_done = [chains[name] for name in ("pa", "pb", "fa", "fb", "wo", "q0")] + list(spread.values())

    def steps(place):
        for name, k in plan[place]:
            if name in spread:
                spread[name].step(k)
            elif name == "sent":
                for each in early_done:
                    each.sent()
            elif k == len(chains[name].stages) - 1:
                last_steps[name]()
            else:
                chains[name].step(k)

    pa_w, pb_w = (row_weights([x for x in order if x != "zh"], 2) for order in (PA_ORDER, PB_ORDER))
    fa_w, fb_w = (row_weights([x for x in order if x != "y"]) for order in (FA_ORDER, FB_ORDER))
    wo_w, q_w = row_weights(WO_ORDER), row_weights(Q_ORDER)

    for n in range(2):
        h = (1 - t2) if n == 0 else t2
        for w in range(2):
            grad = nn(a.dout_t[HALF * w : HALF * w + HALF, :], a.hid[:, part(h, D)]).astype(BF)
            for i in range(2):
                for e in range(2):
                    piece = grad[2 * OWN * e : 2 * OWN * e + 2 * OWN, HALF * i : HALF * i + HALF]
                    at_a = OWN * (pa_w["x"] * i + pa_w["y"] * w + e)
                    at_b = OWN * (pb_w["x"] * i + pb_w["y"] * w + e)
                    a.gpj[at_a : at_a + OWN, pl.ds(pl.multiple_of(D * h, HALF), HALF)] = piece[:OWN]
                    a.gpj[at_b : at_b + OWN, pl.ds(pl.multiple_of(D * h + HALF, HALF), HALF)] = piece[OWN:]
        if n == 0:
            pb.start(0)
    pa.start(0)

    grad_hidden((far, far_p), True)

    def out_of(g):
        return nn(stack_rows(a.hid, spans_of(blocks_of(g))), a.wproj[...])

    def back_of(g):
        return nt(stack_rows(a.gpre, spans_of(blocks_of(g))), a.wfc[...])

    @pl.when(d >= 0)
    def _():
        out, grad = out_of(0), back_of(0)
        for k in range(2):
            a.obuf[k] = out[SPAN * k : SPAN * k + SPAN].astype(BF)
            o_copy(k).start()
        for k in range(2):
            a.gbuf[k] = grad[SPAN * k : SPAN * k + SPAN].astype(BF)
            g_copy(k).start()

    def weights_fc(n):
        h = lax.rem(n, 2)
        w = lax.div(n, 2)
        ones = jnp.ones((16, SEQ), BF)
        grad = nn(jnp.concatenate([a.wqkv[part(h, HALF), :SEQ], ones], axis=0), a.gpre[:, part(w, D)])
        a.acc_bfc[:, part(w, D)] = grad[HALF : HALF + 1]
        grad = grad.astype(BF)
        for j in range(2):
            for i in range(2):
                piece = grad[OWN * (2 * j + i) : OWN * (2 * j + i) + OWN]
                at_a = fa_w["x"] * i + fa_w["zl"] * j + fa_w["zh"] * h
                at_b = fb_w["x"] * i + fb_w["zl"] * j + fb_w["zh"] * h
                a.dout_t[part(at_a, OWN), part(w, HALF)] = piece[:, :HALF]
                a.gfb[part(at_b, OWN), part(w, HALF)] = piece[:, HALF:]

    loop(4, weights_fc)
    fa.start(0)
    fb.start(0)
    for load in loads_qkv:
        load.start()
    steps(("back", 0))

    @pl.when(d >= 0)
    def _():
        grad_in = back_of(1)
        for k in (1, 0):
            t = blocks_of(1)[k]
            normed, inverse = stats(a.gres[k])
            g_copy(k).wait_recv()
            grad = grad_in[SPAN * k : SPAN * k + SPAN] + a.gin[k].astype(F32)
            wide = a.drow[t].astype(F32)
            branch = (wide + norm_back(grad * a.gain_two[...], normed, inverse)).astype(BF)
            a.gbr[t] = branch
            b_copy(k).start()
            a.acc[0] += jnp.sum(branch.astype(F32), axis=0, keepdims=True)
            a.acc[1] += jnp.sum(wide, axis=0, keepdims=True)
            a.acc[4] += jnp.sum(grad * normed, axis=0, keepdims=True)
            a.acc[5] += jnp.sum(grad, axis=0, keepdims=True)

    steps(("back", 1))

    @pl.when(d >= 0)
    def _():
        out = out_of(1)
        for k in (1, 0):
            o_copy(k).wait_recv()
            g_copy(k).wait_send()
            whole = a.gres[k] + (out[SPAN * k : SPAN * k + SPAN] + a.oin[k].astype(F32)) + a.b_proj[...]
            a.gbuf[k] = whole.astype(BF)
            if k == 1:
                y_far.start()
            else:
                y_own.start()


    spread["ve"].start(early_tiles)

    b_copy(0).wait_recv()
    b_copy(1).wait_recv()

    def branch_block(t):
        rows = pl.ds(mul(t, SPAN), SPAN)
        grad = nt(a.wout[pl.ds(half_c, HALF), :], a.gbr[t])
        for p in range(3):
            parts = []
            for e in range(2):
                head = 2 * p + e
                at = slice(HEAD * head, HEAD * head + HEAD)
                inverse = a.linv[head, :, rows]
                piece = grad[at].astype(BF).astype(F32)
                a.delta[head, :, rows] = inverse * jnp.sum(
                    piece * a.o_t[at, rows].astype(F32), axis=0, keepdims=True
                )
                parts.append(piece * inverse)
            scaled = jnp.concatenate(parts, axis=0).astype(BF)
            a.hid[rows, 3 * HALF + 128 * p : 3 * HALF + 128 * p + 128] = scaled.T

    @pl.when(d >= 0)
    def _():
        for t in range(BLOCKS):
            branch_block(t)

    steps("branch")
    for n in range(2):
        lhs = a.o_t[2 * OWN * n : 2 * OWN * n + 2 * OWN, :]
        grad = nn(lhs[:, :SPAN], a.gbr[0])
        for t in range(1, BLOCKS):
            grad += nn(lhs[:, SPAN * t : SPAN * t + SPAN], a.gbr[t])
        grad = grad.astype(BF)
        for i in range(2):
            for w in range(2):
                at = OWN * (wo_w["zl"] * n + wo_w["x"] * i + wo_w["y"] * w)
                a.wout[at : at + OWN, :HALF] = grad[OWN * i : OWN * i + OWN, HALF * w : HALF * w + HALF]
    wo.start(0)

    def between(p, i):
        for value in range(3):
            if plan["pair", value, i]:

                @pl.when(p == value)
                def _():
                    steps(("pair", value, i))

    def backward_pair(p):
        cols = pl.ds(mul(p, 128), 128)
        do_cols = pl.ds(pl.multiple_of(3 * HALF + 128 * p, 128), 128)
        a.k_t[...] = a.kn[:, cols].T
        masks = [lane < HEAD, lane >= HEAD]

        def rows_of(i):
            return slice(SPAN * i, SPAN * i + SPAN)

        def tile(e, i, j):
            n = i * (i + 1) // 2 + j
            if e == 0:
                return a.wproj.at[pl.ds(SPAN * (n % 6), SPAN), pl.ds(SPAN * (n // 6), SPAN)]
            return a.wfc.at[pl.ds(SPAN * (n % 3), SPAN), pl.ds(SPAN * (n // 3), SPAN)]

        def of_head(ref, i, e, at):
            both = ref[rows_of(i), at]
            return jnp.where(masks[e], both, jnp.zeros_like(both))

        @pl.when(p >= 0)
        def _():
            def grad_of(i, e):
                return nt(a.vn[: SPAN * (i + 1), cols], of_head(a.hid, i, e, do_cols))

            combos = itertools.product(reversed(range(BLOCKS)), range(2))
            for (i, e), product in ahead(combos, grad_of):
                head = 2 * p + e
                delta = a.delta[head, :, rows_of(i)]
                for j in range(i + 1):
                    at = base(i) + SPAN * j
                    weights = a.probs[head, at : at + SPAN, :].astype(F32)
                    tile(e, i, j)[...] = (weights * (product[rows_of(j)] - delta)).astype(BF)

        between(p, 3)

        @pl.when(p >= 0)
        def _():

            for i in reversed(range(BLOCKS)):
                parts = []
                for e in range(2):
                    scores = jnp.concatenate([tile(e, i, j)[...] for j in range(i + 1)], axis=0)
                    parts.append(nn(a.k_t[HEAD * e : HEAD * e + HEAD, : SPAN * (i + 1)], scores))
                a.hid[rows_of(i), cols] = (jnp.concatenate(parts, axis=0) * 0.125).T.astype(BF)

            for i in reversed(range(BLOCKS)):
                keys = slice(0, SPAN * (i + 1))
                at = base(i)
                scores = [
                    jnp.concatenate([tile(e, i, j)[...] for j in range(i + 1)], axis=0) for e in range(2)
                ]
                weights = [a.probs[2 * p + e, at : at + SPAN * (i + 1), :] for e in range(2)]
                queries = [of_head(a.qn, i, e, cols) for e in range(2)]
                grads = [of_head(a.hid, i, e, do_cols) for e in range(2)]
                part_k = nn(jnp.concatenate(scores, axis=1), jnp.concatenate(queries, axis=0))
                part_v = nn(jnp.concatenate(weights, axis=1), jnp.concatenate(grads, axis=0))
                if i == BLOCKS - 1:
                    a.dk[...] = part_k
                    a.dv[...] = part_v
                else:
                    a.dk[keys, :] += part_k
                    a.dv[keys, :] += part_v

            at_k = pl.ds(pl.multiple_of(HALF + 128 * p, 128), 128)
            at_v = pl.ds(pl.multiple_of(2 * HALF + 128 * p, 128), 128)
            low_k, low_v = a.dk[...].astype(BF), a.dv[...].astype(BF)
            a.hid[:, at_k] = low_k
            a.hid[:, at_v] = low_v

            both = jnp.concatenate([a.hid[:, cols], a.hid[:, at_k], a.hid[:, at_v]], axis=1)
            ones = jnp.ones((16, SEQ), BF)
            grad = nn(jnp.concatenate([a.ain_t[...], ones], axis=0), both)
            a.acc_qv[0, :, cols] = grad[D : D + 1, :128]
            a.acc_qv[1, :, cols] = grad[D : D + 1, SPAN:]
            grad = grad.astype(BF)
            for h in range(2):
                for j in range(2):
                    for i in range(2):
                        at = (4 * h + 2 * j + i) * OWN
                        to = q_w["zh"] * h + q_w["zl"] * j + q_w["x"] * i
                        a.gpre[OWN * to : OWN * to + OWN, part(p, HALF)] = grad[at : at + OWN]

        for n, (pair, _, _) in enumerate(Q_CHAINS):

            @pl.when(p == pair)
            def _():
                qs[n][0].start(0)

        between(p, -1)

    for p in range(3):
        mix_copy(p).wait_send()
    loop(3, backward_pair)

    a_first = numbers(2)
    for load in loads_qkv:
        load.wait()

    def a_copy(s):
        return remote(a.obuf.at[s], a.oin.at[s], a_first + s, to_core)

    x_far = remote(a.gbuf.at[1], a.gx_out.at[y], numbers(1), to_y)
    x_own = pltpu.make_async_copy(a.gbuf.at[0], a.gx_out.at[y], a.local.at[11])

    def input_pair(g):
        ts = blocks_of(g)
        spans = spans_of(ts)
        part_in = nt(stack_rows(a.hid, spans, slice(0, 3 * HALF)), a.wqkv[...])
        for k in (1, 0):
            half = slice(SPAN * k, SPAN * k + SPAN)
            if g == 0:
                a.obuf[k] = part_in[half].astype(BF)
                a_copy(k).start()
                continue
            normed, inverse = stats(a.xrow[ts[k]].astype(F32))
            a_copy(k).wait_recv()
            grad = part_in[half] + a.oin[k].astype(F32)
            total = a.gbr[ts[k]].astype(F32) + norm_back(grad * a.gain_one[...], normed, inverse)
            a.gbuf[k] = total.astype(BF)
            if k == 1:
                x_far.start()
            else:
                x_own.start()
            a.acc[2] += jnp.sum(grad * normed, axis=0, keepdims=True)
            a.acc[3] += jnp.sum(grad, axis=0, keepdims=True)

    y_far.wait()
    y_own.wait()
    for k in range(2):
        o_copy(k).wait_send()

    for g in range(2):
        input_pair(g)
        steps(("input", g))

    spread["vl"].start(late_tiles)
    steps("last")

    for n, device in enumerate(extra):
        outs = (
            (a.gpj_out, a.xs_pj, a.xr_pj),
            (a.gfc_out, a.xs_fc, a.xr_fc),
            (a.gwo_out, a.xs_wo, a.xr_wo),
        )
        copies = []
        for m, (out, sent, came) in enumerate(outs):
            sent[0] = out[...].astype(BF)
            copies.append((out, sent, came, m))
        a.xs_q[0] = a.gq_out[c].astype(BF)
        copies.append((a.gq_out.at[c], a.xs_q, a.xr_q, 3))
        started = []
        for out, sent, came, m in copies:
            copy = pltpu.make_async_remote_copy(
                src_ref=sent.at[0],
                dst_ref=came.at[n],
                send_sem=a.xsend.at[n, m],
                recv_sem=a.xrecv.at[n, m],
                device_id=device,
                device_id_type=MESH,
            )
            copy.start()
            started.append(copy)
        for (out, sent, came, m), copy in zip(copies, started):
            copy.wait()
            out[...] = (sent[0].astype(F32) + came[n].astype(F32)).astype(out.dtype)
    if extra:
        a.xs_q[0] = a.gq_out[c]
        copy = remote(a.xs_q.at[0], a.xc_q, numbers(1), to_core)
        copy.start()
        copy.wait()
        a.gq_out[other] = a.xc_q[...]

    for copy in pending:
        copy.wait_send()
    for name in ("q1", "q2"):
        chains[name].sent()
    for s in range(2):
        a_copy(s).wait_send()
    b_copy(0).wait_send()
    b_copy(1).wait_send()
    for copy in (x_far, x_own):
        copy.wait()
    assert count[0] <= 120


def finish_kernel(dp, *refs):
    y_in, gx, gq, gwo, gfc, gpj, early, late = refs[:8]
    (y_out, gx_out, gq_out, bq_out, bv_out, gwo_out, bo_out, gfc_out, bf_out, gpj_out) = refs[8:18]
    rest = refs[18:]
    d = lax.axis_index("dp")
    b = lax.axis_index("blk")
    y, c = lax.div(b, 2), lax.rem(b, 2)
    subs = dp // 8
    sub = lax.rem(d, subs)
    rows = D // dp

    def rows_of(v):
        out = v[:rows]
        for n in range(1, subs):
            out = jnp.where(sub == n, v[rows * n : rows * n + rows], out)
        return out

    y_out[...] = y_in[...]
    gx_out[...] = gx[...].astype(F32)

    @pl.when(pl.program_id(0) == 0)
    def _():
        query = [jnp.concatenate([gq[n, p, :, :128] for p in range(3)], axis=1) for n in range(2)]
        key = [jnp.concatenate([gq[n, p, :, 128:256] for p in range(3)], axis=1) for n in range(2)]
        value = [jnp.concatenate([gq[n, p, :, 256:] for p in range(3)], axis=1) for n in range(2)]
        first = jnp.concatenate([query[0], query[1], key[0]], axis=1)
        second = jnp.concatenate([key[1], value[0], value[1]], axis=1)
        full = jnp.where(y == 0, first, second)
        columns = 3 * D // BLOCKS
        full = full.astype(F32)
        gq_out[...] = rows_of(jnp.where(c == 0, full[:, :columns], full[:, columns:]))
        columns = D // BLOCKS
        gwo_out[...] = rows_of(jnp.where(c == 0, gwo[:, :columns], gwo[:, columns:]))
        gfc_out[...] = rows_of(gfc[...])
        cols_ff = 2 * FF // dp
        out = gpj[:, :cols_ff]
        for n in range(1, subs):
            out = jnp.where(sub == n, gpj[:, cols_ff * n : cols_ff * n + cols_ff], out)
        gpj_out[...] = out

        bq_out[...] = late[2, :rows]
        bv_out[...] = late[3, :rows]
        bo_out[...] = early[0, :rows]
        units = 2 * FF // dp
        pieces = [early[4 + n : 5 + n, : min(128, units - 128 * n)] for n in range(-(-units // 128))]
        bf_out[...] = jnp.concatenate(pieces, axis=1)[0]
        for out, v in zip(rest, (early[1], late[0], late[1], early[2], early[3])):
            out[...] = v[:rows]


def body(dp, layer_input, lengths, w_qkv, b_query, b_value, w_out, b_out, w_fc, b_fc, w_proj, b_proj, *more):
    d_out = more[4]
    vectors = (b_query, b_value, b_out, b_proj) + more[:4] + (b_fc,)
    args = (layer_input, lengths, w_qkv, w_out, w_fc, w_proj, d_out) + vectors
    shapes = scratch(dp)
    spaces = [pl.ANY, pltpu.SMEM] + [pl.ANY] * 5 + [pltpu.VMEM] * len(VECTORS)
    in_specs = [pl.BlockSpec(memory_space=space) for space in spaces]
    out_shape = (
        jax.ShapeDtypeStruct((2, SPAN, D), BF),
        jax.ShapeDtypeStruct((2, SPAN, D), BF),
        jax.ShapeDtypeStruct((2, 3, OWN, HALF), BF),
        jax.ShapeDtypeStruct((OWN, HALF), F32),
        jax.ShapeDtypeStruct((OWN, D), F32),
        jax.ShapeDtypeStruct((HALF // 2, HALF), F32),
        jax.ShapeDtypeStruct((8, 128), F32),
        jax.ShapeDtypeStruct((8, 128), F32),
    )
    out_specs = [pl.BlockSpec(memory_space=pl.ANY)] * 2 + [pl.BlockSpec(memory_space=pltpu.VMEM)] * 6
    outs = pl.pallas_call(
        functools.partial(kernel, dp, INPUTS + OUTPUTS + tuple(shapes)),
        out_shape=out_shape,
        in_specs=in_specs,
        out_specs=out_specs,
        scratch_shapes=list(shapes.values()),
        compiler_params=pltpu.CompilerParams(
            collective_id=0, has_side_effects=True, vmem_limit_bytes=63 * 1024 * 1024
        ),
    )(*args)
    rows = D // dp
    line = jax.ShapeDtypeStruct((rows,), F32)
    out_shape = (
        jax.ShapeDtypeStruct((2, SPAN, D), BF),
        jax.ShapeDtypeStruct((2, SPAN, D), F32),
        jax.ShapeDtypeStruct((rows, 3 * D // BLOCKS), F32),
        line,
        line,
        jax.ShapeDtypeStruct((rows, D // BLOCKS), F32),
        line,
        jax.ShapeDtypeStruct((rows, D), F32),
        jax.ShapeDtypeStruct((2 * FF // dp,), F32),
        jax.ShapeDtypeStruct((D // BLOCKS, 2 * FF // dp), F32),
    ) + (line,) * 5

    def specs(arrays):
        by_row = pl.BlockSpec((1, SPAN, D), lambda n: (n, 0, 0))
        return [by_row, by_row] + [
            pl.BlockSpec(v.shape, lambda n, rank=len(v.shape): (0,) * rank) for v in arrays[2:]
        ]

    done = pl.pallas_call(
        functools.partial(finish_kernel, dp),
        grid=(2,),
        out_shape=out_shape,
        in_specs=specs(outs),
        out_specs=specs(out_shape),
        compiler_params=pltpu.CompilerParams(vmem_limit_bytes=63 * 1024 * 1024),
    )(*outs)
    return tuple(done[:9]) + (done[9].T,) + tuple(done[10:])


def solution(mesh):
    rows = P("dp", "blk", None)
    grid = P("dp", "blk")
    line = P("dp")
    in_specs = (rows, P("dp", None)) + (P(),) * 13 + (rows,)
    out_specs = (rows, rows, grid, line, line, grid, line, grid, line, grid) + (line,) * 5
    dp = mesh.shape["dp"]
    return jax.shard_map(
        functools.partial(body, dp),
        mesh=mesh,
        in_specs=in_specs,
        out_specs=out_specs,
        check_vma=False,
    )
```
